256 devices in a mesh: ctx: 64 (over z, y, core), head: 4 (over x).
Axes of the slice: x: 4, y: 4, z: 8, core: 2. Of those that a mesh axis runs over, the one named last changes fastest.
Arguments:
- queries: bfloat16 [16384, 2560], P('ctx', 'head'), may hold values from -90 to 90
- keys: bfloat16 [16384, 512], P('ctx', 'head'), may hold values from -4.5 to 4.5
- block_position: int32 [256], P('ctx'), may hold values from 0 to 255, as said below
- w_gate_q: bfloat16 [4, 640, 128], P('head'), may hold values from -0.25 to 0.25
- w_gate_k: bfloat16 [4, 384, 128], P('head'), may hold values from -0.3125 to 0.3125
Outputs:
- target_map: float32 [256, 4, 256], P('ctx', 'head')
- grad_gate_q: float32 [4, 640, 128], P('head')
- grad_gate_k: float32 [4, 384, 128], P('head')
- mean_loss: float32 [], replicated
The draws below stay inside these ranges and needn't reach their ends.
Inputs may be any that keep to these rules, and one draw needn't show every extreme that they name: `block_position`: each index of ctx holds 4 blocks that lie one after the other in the sequence, in increasing order; the 256 entries name every block once. The runs of indices i and i + 32 of ctx are mirrored: their run numbers (first block divided by 4) add to 63.
All inputs are finite; a program needn't handle non-finite values.
Results may differ from the reference program's by a relative error of at most 0.0038.
The reference program's roundings to bfloat16 on the way (of `pooled_query`, `key_features`, `gate_query` and `gate_key`) count: a program that leaves them out, or rounds other values in their place, can miss the bound.
Values may be sent and summed in bfloat16 or wider, within the bound.
A program may use at most 64 MiB of HBM per device.

```python
import math
import jax
import jax.numpy as jnp
from jax import lax

HD = 128
GQ = 5
KVH = 4
BLK = 64
TOKENS = 16384
QH = 20
BLK_DEV = 4
NBLK = 256
SHARDS = 64


def shared_keys(key):
    block_drift = jax.random.normal(jax.random.fold_in(key, 101), (NBLK, 1, KVH * HD), jnp.float32)
    token_noise = jax.random.normal(jax.random.fold_in(key, 102), (NBLK, BLK, KVH * HD), jnp.float32)
    return jnp.clip(0.8 * block_drift + 0.8 * token_noise, -4.5, 4.5).reshape(TOKENS, KVH * HD)


def draw_keys(key, part):
    shared = shared_keys(key)
    return shared.astype(jnp.bfloat16)


def draw_queries(key, part):
    key = jax.random.fold_in(key, 2)
    channel_mean = jax.random.normal(jax.random.fold_in(key, 11), (1, 1, QH * HD), jnp.float32)
    block_drift = jax.random.normal(jax.random.fold_in(key, 12), (NBLK, 1, QH * HD), jnp.float32)
    token_noise = jax.random.normal(jax.random.fold_in(key, 13), (NBLK, BLK, QH * HD), jnp.float32)
    values = 0.6 * channel_mean + 0.6 * block_drift + 0.7 * token_noise
    return jnp.clip(values.reshape(TOKENS, QH * HD), -5.0, 5.0).astype(jnp.bfloat16)


def draw_block_position(key, part):
    key = jax.random.fold_in(key, 3)
    pair_count = SHARDS // 2
    pair_order = jax.random.permutation(jax.random.fold_in(key, 1), pair_count).astype(jnp.int32)
    flipped = jax.random.randint(jax.random.fold_in(key, 2), (pair_count,), 0, 2).astype(jnp.int32)
    first_runs = jnp.where(flipped == 1, pair_order, SHARDS - 1 - pair_order).astype(jnp.int32)
    second_runs = (SHARDS - 1 - first_runs).astype(jnp.int32)
    shard_order = jnp.concatenate([first_runs, second_runs]).astype(jnp.int32)
    offsets = jnp.arange(BLK_DEV, dtype=jnp.int32)
    return (shard_order[:, None] * BLK_DEV + offsets[None, :]).reshape(-1).astype(jnp.int32)


def shard_levels(key, shape, pieces, smallest, top_value):
    def one(axis_at, shards_of):
        steps = jax.random.uniform(jax.random.fold_in(jax.random.fold_in(key, 6), axis_at), (shards_of,), jnp.float32, smallest / len(pieces), top_value / len(pieces))
        return jnp.repeat(jnp.exp(steps), shape[axis_at] // shards_of).reshape((-1,) + (1,) * (len(shape) - axis_at - 1))

    gain = one(*pieces[0])
    for cut in pieces[1:]:
        gain = gain * one(*cut)
    return gain


def gaussian(key, extent, spread, bound, split=(), kind=jnp.bfloat16):
    loudness = shard_levels(key, extent, split, -0.22, 0.18) if split else 1.0
    values = jax.random.normal(key, extent, jnp.float32) * spread * loudness
    return jnp.minimum(jnp.maximum(values, -bound), bound).astype(kind)


def setup_inputs(seed: int = 0) -> dict:
    seeds = jax.random.split(jax.random.key(seed), 6)
    queries = draw_queries(jax.random.fold_in(seeds[5], 71), 0)
    keys = draw_keys(jax.random.fold_in(seeds[5], 71), 0)
    block_position = draw_block_position(jax.random.fold_in(seeds[5], 71), 0)
    w_gate_q = gaussian(seeds[3], (KVH, GQ * HD, HD), (GQ * HD) ** -0.5, 0.25, ((0, 4),))
    w_gate_k = gaussian(seeds[4], (KVH, 3 * HD, HD), (3 * HD) ** -0.5, 0.3125, ((0, 4),))
    return {"queries": queries, "keys": keys, "block_position": block_position, "w_gate_q": w_gate_q, "w_gate_k": w_gate_k}


MASKED_SCORE = -1e+30

def token_positions(block_position):
    offsets = jnp.arange(BLK, dtype=jnp.int32)
    return (block_position[:, None] * BLK + offsets[None, :]).reshape(-1).astype(jnp.int32)

def attention_blocks(queries, keys, tok_pos, score_scale):
    key_heads = jnp.transpose(keys.reshape(TOKENS, KVH, HD), (1, 0, 2))
    query_heads = jnp.transpose(queries.reshape(NBLK, BLK, KVH, GQ, HD), (2, 0, 1, 3, 4))
    query_pos = tok_pos.reshape(NBLK, BLK)

    def head_map(head_pair):
        query_head, key_head = head_pair
        key_float = key_head.astype(jnp.float32)

        def block_map(block_pair):
            query_block, block_pos = block_pair
            scores = jnp.einsum('rgd,nd->grn', query_block.astype(jnp.float32), key_float) * score_scale
            allowed = tok_pos[None, None, :] <= block_pos[None, :, None]
            scores = jnp.where(allowed, scores, MASKED_SCORE)
            row_top = lax.optimization_barrier(jnp.max(scores, axis=2, keepdims=True))
            row_total = lax.optimization_barrier(jnp.sum(jnp.exp(scores - row_top), axis=2, keepdims=True))
            probs = jnp.exp(scores - row_top) / row_total
            return lax.optimization_barrier(jnp.max(probs.reshape(GQ * BLK, NBLK, BLK), axis=(0, 2)))
        return lax.map(block_map, (query_head, query_pos))
    return lax.map(head_map, (query_heads, key_heads))

def gate_head(pooled_query, key_features, weight_q, weight_k, block_target, allowed, score_scale):
    gate_query = jnp.dot(pooled_query, weight_q, preferred_element_type=jnp.float32).astype(jnp.bfloat16)
    gate_key = jnp.dot(key_features, weight_k, preferred_element_type=jnp.float32).astype(jnp.bfloat16)
    query_float = gate_query.astype(jnp.float32)
    key_float = gate_key.astype(jnp.float32)
    logits = jnp.dot(query_float, key_float.T, precision=lax.Precision.HIGHEST) * score_scale
    logits = jnp.where(allowed, logits, MASKED_SCORE)
    row_top = lax.optimization_barrier(jnp.max(logits, axis=1, keepdims=True))
    log_prob = logits - row_top - jnp.log(lax.optimization_barrier(jnp.sum(jnp.exp(logits - row_top), axis=1, keepdims=True)))
    gate_prob = jnp.exp(log_prob)
    loss = -jnp.sum(jnp.where(allowed, block_target * log_prob, 0.0))
    delta = gate_prob - block_target
    query_delta = jnp.dot(delta, key_float, precision=lax.Precision.HIGHEST) * score_scale
    key_delta = jnp.dot(delta.T, query_float, precision=lax.Precision.HIGHEST) * score_scale
    grad_query = jnp.dot(pooled_query.astype(jnp.float32).T, query_delta, precision=lax.Precision.HIGHEST)
    grad_key = jnp.dot(key_features.astype(jnp.float32).T, key_delta, precision=lax.Precision.HIGHEST)
    return (grad_query, grad_key, loss)

def reference(queries, keys, block_position, w_gate_q, w_gate_k):
    score_scale = 1.0 / math.sqrt(HD)
    tok_pos = token_positions(block_position)
    pooled = attention_blocks(queries, keys, tok_pos, score_scale)
    block_target = pooled / lax.optimization_barrier(jnp.sum(pooled, axis=2, keepdims=True))
    to_global = (block_position[:, None] == jnp.arange(NBLK, dtype=jnp.int32)[None, :]).astype(jnp.float32)
    target_map = jnp.einsum('hbc,cg->bhg', block_target, to_global, precision=lax.Precision.HIGHEST)
    pooled_query = lax.optimization_barrier(jnp.mean(queries.astype(jnp.float32).reshape(NBLK, BLK, KVH, GQ * HD), axis=1)).astype(jnp.bfloat16)
    key_float = keys.astype(jnp.float32).reshape(NBLK, BLK, KVH, HD)
    key_features = jnp.concatenate([lax.optimization_barrier(jnp.max(key_float, axis=1)), lax.optimization_barrier(jnp.min(key_float, axis=1)), lax.optimization_barrier(jnp.mean(key_float, axis=1))], axis=2).astype(jnp.bfloat16)
    allowed = block_position[None, :] <= block_position[:, None]
    results = [gate_head(pooled_query[:, head_index], key_features[:, head_index], w_gate_q[head_index], w_gate_k[head_index], block_target[head_index], allowed, score_scale) for head_index in range(KVH)]
    grad_gate_q = jnp.stack([result_tuple[0] for result_tuple in results])
    grad_gate_k = jnp.stack([result_tuple[1] for result_tuple in results])
    mean_loss = jnp.sum(jnp.stack([result_tuple[2] for result_tuple in results])) / (KVH * NBLK)
    return (target_map, grad_gate_q, grad_gate_k, mean_loss)
```

```python
import functools
import math

import jax
import jax.numpy as jnp
from jax import lax
from jax.experimental import pallas as pl
from jax.experimental.pallas import tpu as pltpu
from jax.sharding import PartitionSpec as P

ZS, YS, XS = 8, 4, 4
BLK, HD, GQ = 64, 128, 5
TOK = 256
HALF = 128
ROWS = HALF + 16
NEG = -1e30
LOG2E = 1.4426950408889634
SCALE = 1.0 / math.sqrt(HD)
F32, BF16 = jnp.float32, jnp.bfloat16
MESH = pl.DeviceIdType.MESH


def nt(a, b):
    return lax.dot_general(a, b, (((1,), (1,)), ((), ())), preferred_element_type=F32)


def tn(a, b):
    return lax.dot_general(a, b, (((0,), (0,)), ((), ())), preferred_element_type=F32)


def mm(a, b):
    return jnp.dot(a, b, preferred_element_type=F32)


def split2(a):
    hi = a.astype(BF16)
    return hi, (a - hi.astype(F32)).astype(BF16)


def split3(a):
    hi, mid = split2(a)
    return hi, mid, (a - hi.astype(F32) - mid.astype(F32)).astype(BF16)


def iota(shape, dim):
    return lax.broadcasted_iota(jnp.int32, shape, dim)


def kernel(
    q_ref, k_ref, pos_ref, wq_ref, wk_ref,
    map_ref, gq_ref, gk_ref, loss_ref,
    k0, k1, qt, bm8, bmd, m8, l8, posv, kfb, pqb, posi, posii, u8, tb, lx,
    s_y0, s_z0, s_s0, s_z1, s_y1, s_s1, s_t, s_ts, s_x,
    r_y0, r_z0, r_s0, r_z1, r_y1, r_s1, r_t, r_ts, r_x,
):
    ctx, x = lax.axis_index("ctx"), lax.axis_index("head")
    c = lax.rem(ctx, 2)
    y = lax.rem(ctx // 2, YS)
    z = ctx // (2 * YS)

    def zz(d):
        return lax.rem(z + (d + ZS), ZS)

    def yy(d):
        return lax.rem(y + d, YS)

    def dev(z_at, y_at, c_at):
        return ((z_at * YS + y_at) * 2 + c_at, x)

    up, down, sib = dev(zz(1), y, c), dev(zz(-1), y, c), dev(z, y, 1 - c)
    y_peers = [dev(z, yy(d), c) for d in (1, 2, 3)]
    x_peers = [(ctx, lax.rem(x + d, XS)) for d in (1, 2, 3)]

    barrier = pltpu.get_barrier_semaphore()
    peers = [up, down, sib] + y_peers + x_peers
    for peer in peers:
        pl.semaphore_signal(barrier, inc=1, device_id=peer, device_id_type=MESH)

    def send(src, dst, s_sem, r_sem, to):
        pltpu.make_async_remote_copy(
            src_ref=src, dst_ref=dst, send_sem=s_sem, recv_sem=r_sem,
            device_id=to, device_id_type=MESH,
        ).start()

    def wait(like, sem):
        pltpu.make_async_copy(like, like, sem).wait()

    first = pos_ref[0].astype(F32)
    row16 = iota((16, TOK), 0)
    tok16 = iota((16, TOK), 1)
    for half, buf in ((0, k0), (1, k1)):
        pooled = jnp.zeros((16, HD), F32)
        for g in range(GQ):
            pick = (row16 // 2 == g) & (tok16 // BLK == half * 2 + row16 % 2)
            weight = jnp.where(pick, 1.0 / BLK, 0.0).astype(BF16)
            pooled = pooled + mm(weight, q_ref[:, g * HD : (g + 1) * HD])
        pooled = jnp.where(iota((16, HD), 0) >= 10, first, pooled)
        buf[c, z, y, 0:HALF, :] = k_ref[half * HALF : (half + 1) * HALF, :]
        buf[c, z, y, HALF:ROWS, :] = pooled.astype(BF16)

    pl.semaphore_wait(barrier, len(peers))

    own0, own1 = k0.at[c, z, y], k1.at[c, z, y]
    for n, peer in enumerate(y_peers):
        send(own0, own0, s_y0, r_y0.at[n], peer)
    for n, peer in ((0, up), (1, down)):
        send(own1, own1, s_z1, r_z1.at[1, n], peer)
    for n, peer in ((0, up), (1, down)):
        send(own0, own0, s_z0, r_z0.at[1, n, y // 2], peer)
    for peer in y_peers:
        send(own1, own1, s_y1, r_y1.at[z], peer)

    for g in range(GQ):
        scaled = (q_ref[:, g * HD : (g + 1) * HD].astype(F32) * (SCALE * LOG2E)).T
        hi, lo = split2(scaled)
        qt[g, 0:HD, :] = hi
        qt[g, HD : 2 * HD, :] = lo

    own_kk = jnp.concatenate([k_ref[...], k_ref[...]], axis=1)
    causal = iota((TOK, TOK), 0) <= iota((TOK, TOK), 1)
    for g in range(GQ):
        s = jnp.where(causal, mm(own_kk, qt[g]), NEG)
        m = jnp.max(s.reshape(4, 8, 8, TOK), axis=1)
        bmd[g] = m.reshape(32, TOK)
        top = jnp.max(m, axis=0)
        m8[g] = top
        l8[g] = jnp.sum(jnp.exp2(s.reshape(32, 8, TOK) - top[None]), axis=0)

    def z_pass(k, n):
        src_z = zz(-k) if n == 0 else zz(k)
        part = k1.at[c, src_z, y]
        wait(part, r_z1.at[k, n])
        if k < 3:
            send(part, part, s_z1, r_z1.at[k + 1, n], up if n == 0 else down)
        elif k == 3:
            @pl.when(c == n)
            def _():
                send(part, part, s_z1, r_z1.at[4, 0], up if n == 0 else down)
        for peer in y_peers:
            send(part, part, s_y1, r_y1.at[src_z], peer)

    def y_done(d):
        at = zz(d)
        wait(k1.at[c, at, 0:3], r_y1.at[at])
        send(k1.at[c, at], k1.at[c, at], s_s1, r_s1.at[at], sib)

    def bundle_pass(k, n):
        src_z = zz(-k) if n == 0 else zz(k)
        for pair in range(2):
            part = k0.at[c, src_z, 2 * pair : 2 * pair + 2]
            wait(part, r_z0.at[k, n, pair])
            if k < 3:
                send(part, part, s_z0, r_z0.at[k + 1, n, pair], up if n == 0 else down)
            elif k == 3:
                @pl.when(c == n)
                def _(part=part, pair=pair):
                    send(part, part, s_z0, r_z0.at[4, 0, pair], up if n == 0 else down)
        whole = k0.at[c, src_z]
        send(whole, whole, s_s0, r_s0.at[src_z], sib)

    for n in range(2):
        z_pass(1, n)
    for n, d in enumerate((3, 2, 1)):
        part = k0.at[c, z, yy(d)]
        wait(part, r_y0.at[n])
        for m, peer in ((0, up), (1, down)):
            send(part, part, s_z0, r_z0.at[1, m, yy(d) // 2], peer)
    send(k0.at[c, z], k0.at[c, z], s_s0, r_s0.at[z], sib)
    y_done(0)

    def z_last():
        part = k1.at[c, zz(4), y]
        wait(part, r_z1.at[4, 0])
        for peer in y_peers:
            send(part, part, s_y1, r_y1.at[zz(4)], peer)

    def bundle_last():
        for pair in range(2):
            wait(k0.at[c, zz(4), 2 * pair : 2 * pair + 2], r_z0.at[4, 0, pair])
        whole = k0.at[c, zz(4)]
        send(whole, whole, s_s0, r_s0.at[zz(4)], sib)

    events = {
        0: lambda: [z_pass(2, n) for n in range(2)],
        1: lambda: [y_done(d) for d in (-1, 1)],
        2: lambda: [bundle_pass(1, n) for n in range(2)] + [z_pass(3, n) for n in range(2)],
        3: lambda: [y_done(d) for d in (-2, 2)],
        4: lambda: z_last(),
        5: lambda: [y_done(d) for d in (-3, 3)],
        6: lambda: [bundle_pass(2, n) for n in range(2)],
        8: lambda: y_done(4),
        10: lambda: [bundle_pass(3, n) for n in range(2)],
        14: lambda: bundle_last(),
    }

    def at_slot(slot, which):
        for number, event in events.items():
            if number % 2 == which:
                @pl.when(slot == number)
                def _(event=event):
                    event()

    bufs = (k0, k1)

    def chunk(i, _):
        step = (i + 1) // 2
        zi = lax.rem(z + ZS + jnp.where(lax.rem(i, 2) == 1, -step, step), ZS)
        at_slot(2 * i, 0)
        wait(k0.at[1 - c, zi], r_s0.at[zi])
        wait(k1.at[1 - c, zi], r_s1.at[zi])
        pieces = []
        for half in range(2):
            for cc in range(2):
                piece = bufs[half][cc, zi, :, 0:HALF, :].reshape(YS * HALF, HD)
                wide = piece.astype(F32).reshape(8, BLK, HD)
                kfb[half, cc, zi, :, 0:HD] = jnp.max(wide, axis=1)
                kfb[half, cc, zi, :, HD : 2 * HD] = jnp.min(wide, axis=1)
                kfb[half, cc, zi, :, 2 * HD : 3 * HD] = jnp.sum(wide, axis=1) * (1.0 / BLK)
                pieces.append(piece)
        for cc in range(2):
            for yi in range(YS):
                mark = k0[cc, zi, yi, HALF:ROWS, :].astype(F32)[10:11, :]
                posv[cc * YS + yi] = jnp.broadcast_to(mark, (8, HD))
        keys = jnp.concatenate(pieces, axis=0)
        kk = jnp.concatenate([keys, keys], axis=1)
        for g in range(GQ):
            if g == 3:
                at_slot(2 * i + 1, 1)
            s = mm(kk, qt[g])
            top, total = m8[g], l8[g]
            for half in range(2):
                for cc in range(2):
                    base = pl.multiple_of((half * 128 + (cc * ZS + zi) * 8) * 8, 64)
                    for blk in range(8):
                        r0 = (half * 2 + cc) * 512 + blk * BLK
                        sb = s[r0 : r0 + BLK].reshape(8, 8, TOK)
                        mark = posv[cc * YS + blk // 2] < first
                        ok = jnp.concatenate([mark, mark], axis=1)
                        m = jnp.where(ok, jnp.max(sb, axis=0), NEG)
                        bm8[g, pl.ds(base + blk * 8, 8), :] = m
                        new = jnp.maximum(top, m)
                        part = jnp.sum(jnp.exp2(sb - new[None]), axis=0)
                        total = total * jnp.exp2(top - new) + jnp.where(ok, part, 0.0)
                        top = new
            m8[g] = top
            l8[g] = total
        return 0

    lax.fori_loop(0, ZS, chunk, 0)

    own = ((c * ZS + z) * YS + y) * 2
    for half in range(2):
        at = pl.multiple_of((half * 128 + own) * 8, 16)
        for g in range(GQ):
            bm8[g, pl.ds(at, 16), :] = bmd[g, half * 16 : half * 16 + 16, :]

    offs = []
    for g in range(GQ):
        m = jnp.max(m8[g], axis=0, keepdims=True)
        total = jnp.sum(l8[g] * jnp.exp2(m8[g] - m), axis=0, keepdims=True)
        offs.append(jnp.broadcast_to(m + jnp.log(total) * LOG2E, (8, TOK)))

    def merge(i, _):
        at = pl.multiple_of(i * 64, 64)
        best = None
        for g in range(GQ):
            v = bm8[g, pl.ds(at, 64), :].reshape(8, 8, TOK) - offs[g][None]
            best = v if best is None else jnp.maximum(best, v)
        best = best.reshape(64, TOK)
        for n in range(2):
            u8[n, pl.ds(at, 64), :] = best[:, n * 128 : (n + 1) * 128]
        return 0

    lax.fori_loop(0, 32, merge, 0, unroll=4)
    halves = []
    for n in range(2):
        r = u8[n, pl.ds(0, 256, stride=8), :]
        for t in range(1, 8):
            r = jnp.maximum(r, u8[n, pl.ds(t, 256, stride=8), :])
        halves.append(r.T)
    best = jnp.concatenate(halves, axis=0)
    prob = jnp.exp2(jnp.max(best.reshape(4, BLK, 256), axis=1))
    target = prob / jnp.sum(prob, axis=1, keepdims=True)
    me = z * YS + y
    tb[c, me, 0:4, :] = target[:, 0:128]
    tb[c, me, 4:8, :] = target[:, 128:256]
    mine = tb.at[c, me]
    for dz in (4, 3, 5, 2, 6, 1, 7, 0):
        for dy in (2, 1, 3, 0):
            if dz or dy:
                send(mine, mine, s_t, r_t, dev(zz(dz), yy(dy), c))

    o, kr = iota((112, 128), 0), iota((112, 128), 1)
    b = o % 4
    want_q = (b // 2) * 64 + (o % 16) // 4 * 16 + (o // 16) * 2 + b % 2
    want_i = (o % 16) // 4 * 16 + 10
    want_ii = (o % 8) // 2 * 16 + 10
    want = jnp.where(o < 80, want_q, jnp.where(o < 96, want_i, want_ii))
    pick = jnp.where(kr == want, 1.0, 0.0).astype(BF16)

    def unpack(i, _):
        cc, zi = i // ZS, lax.rem(i, ZS)
        rows = jnp.concatenate(
            [bufs[half][cc, zi, :, HALF:ROWS, :].reshape(64, HD) for half in range(2)], axis=0
        )
        got = mm(pick, rows)
        for g in range(GQ):
            pqb[g, i] = got[g * 16 : (g + 1) * 16].astype(BF16)
        posi[i] = got[80:96] + (iota((16, HD), 0) % 4).astype(F32)
        for half in range(2):
            at = 96 + half * 8
            posii[half, i] = got[at : at + 8] + (iota((8, HD), 0) % 2 + half * 2).astype(F32)
        return 0

    lax.fori_loop(0, 16, unpack, 0, unroll=4)
    pos_row = posi[...].reshape(256, HD)
    pos_col = posii[...].reshape(256, HD)
    pos_row = jnp.concatenate([pos_row, pos_row], axis=1)
    place = jnp.where(
        jnp.concatenate([pos_col, pos_col], axis=1) == iota((256, 256), 1).astype(F32), 1.0, 0.0
    ).astype(BF16)
    full = jnp.zeros((8, 256), F32)
    for term in split3(jnp.concatenate([target, target], axis=0)):
        full = full + mm(term, place)
    for n in range(4):
        map_ref[n] = full[n : n + 1]
    feats = kfb[...].reshape(256, 3 * HD).astype(BF16)
    pooled = [pqb[g].reshape(256, HD) for g in range(GQ)]
    gate_q = jnp.zeros((256, HD), F32)
    for g in range(GQ):
        gate_q = gate_q + mm(pooled[g], wq_ref[0, g * HD : (g + 1) * HD, :])
    gate_q = gate_q.astype(BF16)
    gate_k = mm(feats, wk_ref[0]).astype(BF16)
    allowed = jnp.broadcast_to(pos_col.T[0:1, :], (256, 256)) <= pos_row
    logits = jnp.where(allowed, nt(gate_q, gate_k) * SCALE, NEG)
    shifted = logits - jnp.max(logits, axis=1, keepdims=True)
    log_prob = shifted - jnp.log(jnp.sum(jnp.exp(shifted), axis=1, keepdims=True))
    gate_prob = jnp.exp(log_prob)

    wait(tb.at[c, 0:31], r_t)
    send(tb.at[c], tb.at[c], s_ts, r_ts, sib)
    wait(tb.at[1 - c], r_ts)
    tiles = tb[...].reshape(32, 2, 8, 128)
    even, odd = tiles[:, 0], tiles[:, 1]
    low = iota((32, 8, 128), 1) < 4
    left = jnp.where(low, even, pltpu.roll(odd, 4, 1))
    right = jnp.where(low, pltpu.roll(even, 4, 1), odd)
    targets = jnp.concatenate([left.reshape(256, 128), right.reshape(256, 128)], axis=1)
    loss = -jnp.sum(jnp.where(allowed, targets * log_prob, 0.0), axis=0, keepdims=True)
    loss = jnp.sum(loss, axis=1, keepdims=True)
    lx[x] = jnp.broadcast_to(loss, (8, 128))
    for n, peer in enumerate(x_peers):
        send(lx.at[x], lx.at[x], s_x.at[n], r_x.at[n], peer)
    delta = (gate_prob - targets) * SCALE
    d_hi, d_lo = split2(delta)
    q_delta = jnp.concatenate(split2(mm(d_hi, gate_k) + mm(d_lo, gate_k)), axis=1)
    k_delta = jnp.concatenate(split2(tn(d_hi, gate_q) + tn(d_lo, gate_q)), axis=1)
    for g in range(GQ):
        both = tn(pooled[g], q_delta)
        gq_ref[0, g * HD : (g + 1) * HD, :] = both[:, 0:HD] + both[:, HD:]
    both = tn(feats, k_delta)
    gk_ref[0] = both[:, 0:HD] + both[:, HD:]
    for n, d in enumerate((1, 2, 3)):
        at = lax.rem(x + XS - d, XS)
        wait(lx.at[at], r_x.at[n])
    loss_ref[...] = (lx[0] + lx[1] + lx[2] + lx[3])[0:1, 0:1] * (1.0 / (256 * XS))

    wait(k0.at[c, 0, 0:3], s_y0)
    wait(k0.at[c, 0:7], s_z0)
    wait(k0.at[c], s_s0)
    wait(k1.at[c, 0:7, 0], s_z1)
    wait(k1.at[c, 0:6], s_y1)
    wait(k1.at[c], s_s1)
    wait(tb.at[c, 0:31], s_t)
    wait(tb.at[c], s_ts)
    for n in range(3):
        wait(lx.at[x], s_x.at[n])


def per_device(queries, keys, block_position, w_gate_q, w_gate_k):
    vmem = pl.BlockSpec(memory_space=pltpu.VMEM)
    smem = pl.BlockSpec(memory_space=pltpu.SMEM)
    dma = pltpu.SemaphoreType.DMA
    target_map, grad_q, grad_k, loss = pl.pallas_call(
        kernel,
        out_shape=(
            jax.ShapeDtypeStruct((4, 1, 256), F32),
            jax.ShapeDtypeStruct((1, GQ * HD, HD), F32),
            jax.ShapeDtypeStruct((1, 3 * HD, HD), F32),
            jax.ShapeDtypeStruct((1, 1), F32),
        ),
        in_specs=[vmem, vmem, smem, vmem, vmem],
        out_specs=(vmem, vmem, vmem, vmem),
        scratch_shapes=[
            pltpu.VMEM((2, ZS, YS, ROWS, HD), BF16),
            pltpu.VMEM((2, ZS, YS, ROWS, HD), BF16),
            pltpu.VMEM((GQ, 2 * HD, TOK), BF16),
            pltpu.VMEM((GQ, 2048, TOK), F32),
            pltpu.VMEM((GQ, 32, TOK), F32),
            pltpu.VMEM((GQ, 8, TOK), F32),
            pltpu.VMEM((GQ, 8, TOK), F32),
            pltpu.VMEM((8, 8, HD), F32),
            pltpu.VMEM((2, 2, ZS, 8, 3 * HD), F32),
            pltpu.VMEM((GQ, 16, 16, HD), BF16),
            pltpu.VMEM((16, 16, HD), F32),
            pltpu.VMEM((2, 16, 8, HD), F32),
            pltpu.VMEM((2, 2048, 128), F32),
            pltpu.VMEM((2, 32, 8, 128), F32),
            pltpu.VMEM((XS, 8, 128), F32),
            dma, dma, dma, dma, dma, dma, dma, dma, dma((3,)),
            dma((3,)), dma((5, 2, 2)), dma((ZS,)), dma((5, 2)), dma((ZS,)), dma((ZS,)),
            dma, dma, dma((3,)),
        ],
        compiler_params=pltpu.CompilerParams(
            collective_id=0, has_side_effects=True, vmem_limit_bytes=50 << 20
        ),
        name="gate",
    )(queries, keys, block_position, w_gate_q, w_gate_k)
    return target_map, grad_q, grad_k, loss.reshape(())


def solution(mesh):
    return jax.shard_map(
        per_device,
        mesh=mesh,
        in_specs=(
            P("ctx", "head"),
            P("ctx", "head"),
            P("ctx"),
            P("head", None, None),
            P("head", None, None),
        ),
        out_specs=(P("ctx", "head", None), P("head", None, None), P("head", None, None), P()),
        check_vma=False,
    )
```

```python
import functools
import math

import jax
import jax.numpy as jnp
from jax import lax
from jax.experimental import pallas as pl
from jax.experimental.pallas import tpu as pltpu
from jax.sharding import PartitionSpec as P

ZS, YS, XS = 8, 4, 4
BLK, HD, GQ = 64, 128, 5
TOK = 256
HALF = 128
ROWS = HALF + 16
NEG = -1e30
LOG2E = 1.4426950408889634
SCALE = 1.0 / math.sqrt(HD)
F32, BF16 = jnp.float32, jnp.bfloat16
MESH = pl.DeviceIdType.MESH


def nt(a, b):
    return lax.dot_general(a, b, (((1,), (1,)), ((), ())), preferred_element_type=F32)


def tn(a, b):
    return lax.dot_general(a, b, (((0,), (0,)), ((), ())), preferred_element_type=F32)


def mm(a, b):
    return jnp.dot(a, b, preferred_element_type=F32)


def split2(a):
    hi = a.astype(BF16)
    return hi, (a - hi.astype(F32)).astype(BF16)


def split3(a):
    hi, mid = split2(a)
    return hi, mid, (a - hi.astype(F32) - mid.astype(F32)).astype(BF16)


def iota(shape, dim):
    return lax.broadcasted_iota(jnp.int32, shape, dim)


def kernel(
    q_hbm, k_hbm, pos_ref, wq_hbm, wk_hbm,
    map_hbm, gq_hbm, gk_hbm, loss_ref,
    map_ref, gq_ref, gk_ref, s_out,
    q_ref, k_ref, wq_ref, wk_ref,
    k0, k1, qt, bm8, bmd, m8, l8, posv, kfb, pqb, posi, posii, u8, tb, lx, lp, gp, gqv, s_in,
    s_y0, s_z0, s_s0, s_z1, s_y1, s_s1, s_t, s_ts, s_x,
    r_y0, r_z0, r_s0, r_z1, r_y1, r_s1, r_t, r_ts, r_x,
):
    ctx, x = lax.axis_index("ctx"), lax.axis_index("head")
    c = lax.rem(ctx, 2)
    y = lax.rem(ctx // 2, YS)
    z = ctx // (2 * YS)

    def zz(d):
        return lax.rem(z + (d + ZS), ZS)

    def yy(d):
        return lax.rem(y + d, YS)

    def dev(z_at, y_at, c_at):
        return ((z_at * YS + y_at) * 2 + c_at, x)

    up, down, sib = dev(zz(1), y, c), dev(zz(-1), y, c), dev(z, y, 1 - c)
    y_peers = [dev(z, yy(d), c) for d in (1, 2, 3)]
    other = ctx + 1 - 2 * c
    x_peers = [(at, lax.rem(x + d, XS)) for d in (1, 2, 3) for at in (ctx, other)]

    mine0, mine1 = k0.at[c, z, y], k1.at[c, z, y]
    own0, own1 = mine0.at[0:HALF], mine1.at[0:HALF]
    tile0, tile1 = mine0.at[HALF:ROWS], mine1.at[HALF:ROWS]
    keys0, keys1 = k_hbm.at[0:HALF], k_hbm.at[HALF:TOK]
    loads = [
        pltpu.make_async_copy(src, dst, s_in.at[n])
        for n, (src, dst) in enumerate(
            (
                (q_hbm, q_ref), (k_hbm, k_ref), (keys0, own0), (keys1, own1),
                (wq_hbm, wq_ref), (wk_hbm, wk_ref),
            )
        )
    ]
    for load in loads:
        load.start()
    barrier = pltpu.get_barrier_semaphore()
    peers = [up, down, sib] + y_peers + x_peers
    for peer in peers:
        pl.semaphore_signal(barrier, inc=1, device_id=peer, device_id_type=MESH)

    def send(src, dst, s_sem, r_sem, to):
        pltpu.make_async_remote_copy(
            src_ref=src, dst_ref=dst, send_sem=s_sem, recv_sem=r_sem,
            device_id=to, device_id_type=MESH,
        ).start()

    def wait(like, sem):
        pltpu.make_async_copy(like, like, sem).wait()

    def send_own(src0, dst0, src1, dst1):
        for n, peer in enumerate(y_peers):
            send(src0, dst0, s_y0, r_y0.at[n], peer)
        for n, peer in ((0, up), (1, down)):
            send(src1, dst1, s_z1, r_z1.at[1, n], peer)
        for n, peer in ((0, up), (1, down)):
            send(src0, dst0, s_z0, r_z0.at[1, n, y // 2], peer)
        for peer in y_peers:
            send(src1, dst1, s_y1, r_y1.at[z], peer)

    pl.semaphore_wait(barrier, len(peers))
    send_own(keys0, own0, keys1, own1)

    first = pos_ref[0].astype(F32)
    loads[0].wait()
    row16 = iota((16, TOK), 0)
    tok16 = iota((16, TOK), 1)
    for half, tile in ((0, tile0), (1, tile1)):
        pooled = jnp.zeros((16, HD), F32)
        for g in range(GQ):
            pick = (row16 // 2 == g) & (tok16 // BLK == half * 2 + row16 % 2)
            weight = jnp.where(pick, 1.0 / BLK, 0.0).astype(BF16)
            pooled = pooled + mm(weight, q_ref[:, g * HD : (g + 1) * HD])
        pooled = jnp.where(iota((16, HD), 0) >= 10, first, pooled)
        tile[...] = pooled.astype(BF16)
    send_own(tile0, tile0, tile1, tile1)

    for g in range(GQ):
        scaled = (q_ref[:, g * HD : (g + 1) * HD].astype(F32) * (SCALE * LOG2E)).T
        hi, lo = split2(scaled)
        qt[g, 0:HD, :] = hi
        qt[g, HD : 2 * HD, :] = lo

    for n in (1, 2, 3):
        loads[n].wait()
    own_kk = jnp.concatenate([k_ref[...], k_ref[...]], axis=1)
    causal = iota((TOK, TOK), 0) <= iota((TOK, TOK), 1)
    for g in range(GQ):
        s = jnp.where(causal, mm(own_kk, qt[g]), NEG)
        m = jnp.max(s.reshape(4, 8, 8, TOK), axis=1)
        bmd[g] = m.reshape(32, TOK)
        top = jnp.max(m, axis=0)
        m8[g] = top
        l8[g] = jnp.sum(jnp.exp2(s.reshape(32, 8, TOK) - top[None]), axis=0)

    def z_pass(k):
        for n, src_z in ((0, zz(-k)), (1, zz(k))):
            part = k1.at[c, src_z, y]
            wait(part, r_z1.at[k, n])
            if k < 3:
                send(part, part, s_z1, r_z1.at[k + 1, n], up if n == 0 else down)
            else:
                @pl.when(c == n)
                def _(part=part, n=n):
                    send(part, part, s_z1, r_z1.at[4, 0], up if n == 0 else down)
            for peer in y_peers:
                send(part, part, s_y1, r_y1.at[src_z], peer)

    def y_done(d):
        at = zz(d)
        wait(k1.at[c, at, 0:3], r_y1.at[at])
        send(k1.at[c, at], k1.at[c, at], s_s1, r_s1.at[at], sib)

    def bundle_pass(k, p):
        pair = lax.rem(y // 2 + p, 2)
        for n, src_z in ((0, zz(-k)), (1, zz(k))):
            part = k0.at[c, src_z, pl.ds(2 * pair, 2)]
            wait(part, r_z0.at[k, n, pair])
            if k < 3:
                send(part, part, s_z0, r_z0.at[k + 1, n, pair], up if n == 0 else down)
            else:
                @pl.when(c == n)
                def _(part=part, n=n):
                    send(part, part, s_z0, r_z0.at[4, 0, pair], up if n == 0 else down)
        if p == 1:
            for src_z in (zz(-k), zz(k)):
                send(k0.at[c, src_z], k0.at[c, src_z], s_s0, r_s0.at[src_z], sib)

    def bundle_last():
        for pair in range(2):
            wait(k0.at[c, zz(4), 2 * pair : 2 * pair + 2], r_z0.at[4, 0, pair])
        whole = k0.at[c, zz(4)]
        send(whole, whole, s_s0, r_s0.at[zz(4)], sib)

    def z_last():
        part = k1.at[c, zz(4), y]
        wait(part, r_z1.at[4, 0])
        for peer in y_peers:
            send(part, part, s_y1, r_y1.at[zz(4)], peer)

    def y_pass(d):
        part = k0.at[c, z, yy(d)]
        wait(part, r_y0.at[3 - d])
        for n, peer in ((0, up), (1, down)):
            send(part, part, s_z0, r_z0.at[1, n, yy(d) // 2], peer)

    y_pass(3)
    y_pass(1)
    z_pass(1)
    y_pass(2)
    send(k0.at[c, z], k0.at[c, z], s_s0, r_s0.at[z], sib)
    y_done(0)

    bufs = (k0, k1)

    def attend(cc, zs):
        pieces = []
        for half in range(2):
            for zi in zs:
                piece = bufs[half][cc, zi, :, 0:HALF, :].reshape(YS * HALF, HD)
                wide = piece.astype(F32).reshape(8, BLK, HD)
                kfb[half, cc, zi, :, 0:HD] = jnp.max(wide, axis=1)
                kfb[half, cc, zi, :, HD : 2 * HD] = jnp.min(wide, axis=1)
                kfb[half, cc, zi, :, 2 * HD : 3 * HD] = jnp.sum(wide, axis=1) * (1.0 / BLK)
                pieces.append(piece)
        for n, zi in enumerate(zs):
            for yi in range(YS):
                mark = k0[cc, zi, yi, HALF:ROWS, :].astype(F32)[10:11, :]
                posv[n * YS + yi] = jnp.broadcast_to(mark, (8, HD))
        keys = jnp.concatenate(pieces, axis=0)
        kk = jnp.concatenate([keys, keys], axis=1)
        for g in range(GQ):
            s = mm(kk, qt[g])
            for side in range(2):
                cols = slice(side * 128, side * 128 + 128)
                top, total = m8[g, :, cols], l8[g, :, cols]
                for half in range(2):
                    for n, zi in enumerate(zs):
                        base = pl.multiple_of((half * 128 + (cc * ZS + zi) * 8) * 8, 64)
                        for yi in range(YS):
                            r0 = ((half * len(zs) + n) * YS + yi) * HALF
                            sb = s[r0 : r0 + HALF, cols].reshape(16, 8, 128)
                            ok = posv[n * YS + yi] < first
                            new = top
                            for blk in range(2):
                                m = jnp.max(sb[blk * 8 : blk * 8 + 8], axis=0)
                                m = jnp.where(ok, m, NEG)
                                bm8[g, pl.ds(base + (yi * 2 + blk) * 8, 8), cols] = m
                                new = jnp.maximum(new, m)
                            part = jnp.sum(jnp.exp2(sb - new[None]), axis=0)
                            total = total * jnp.exp2(top - new) + jnp.where(ok, part, 0.0)
                            top = new
                m8[g, :, cols] = top
                l8[g, :, cols] = total

    def both_cores(d):
        def one(j, _):
            cc = lax.rem(c + j, 2)

            @pl.when(j == 1)
            def _():
                if d == 0:
                    bundle_pass(1, 0)
                    z_pass(2)
                wait(k0.at[1 - c, zz(d)], r_s0.at[zz(d)])
                wait(k1.at[1 - c, zz(d)], r_s1.at[zz(d)])

            attend(cc, [zz(d)])
            return 0

        lax.fori_loop(0, 2, one, 0)

    def at_step(i, events):
        for number, event in events.items():
            @pl.when(i == number)
            def _(event=event):
                event()

    def pair_step(i, _):
        k, j = i // 2 + 1, lax.rem(i, 2)
        cc = lax.rem(c + j, 2)
        zs = [lax.rem(z + ZS - k, ZS), lax.rem(z + k, ZS)]
        at_step(i, {
            0: lambda: [bundle_pass(1, 1)] + [y_done(d) for d in (-1, 1)],
            1: lambda: [bundle_pass(2, 0), z_pass(3)],
            2: lambda: [bundle_pass(2, 1)] + [y_done(d) for d in (-2, 2)],
            3: lambda: [bundle_pass(3, 0), z_last()],
            4: lambda: [y_done(d) for d in (-3, 3)] + [bundle_pass(3, 1)],
            5: lambda: y_done(4),
        })

        @pl.when(j == 1)
        def _():
            for zi in zs:
                wait(k0.at[1 - c, zi], r_s0.at[zi])
                wait(k1.at[1 - c, zi], r_s1.at[zi])

        attend(cc, zs)
        return 0

    both_cores(0)
    lax.fori_loop(0, 6, pair_step, 0)
    bundle_last()
    both_cores(4)

    own = ((c * ZS + z) * YS + y) * 2
    for half in range(2):
        at = pl.multiple_of((half * 128 + own) * 8, 16)
        for g in range(GQ):
            bm8[g, pl.ds(at, 16), :] = bmd[g, half * 16 : half * 16 + 16, :]

    offs = []
    for g in range(GQ):
        m = jnp.max(m8[g], axis=0, keepdims=True)
        total = jnp.sum(l8[g] * jnp.exp2(m8[g] - m), axis=0, keepdims=True)
        offs.append(jnp.broadcast_to(m + jnp.log(total) * LOG2E, (8, TOK)))

    def merge(i, _):
        at = pl.multiple_of(i * 64, 64)
        best = None
        for g in range(GQ):
            v = bm8[g, pl.ds(at, 64), :].reshape(8, 8, TOK) - offs[g][None]
            best = v if best is None else jnp.maximum(best, v)
        best = best.reshape(64, TOK)
        for n in range(2):
            u8[n, pl.ds(at, 64), :] = best[:, n * 128 : (n + 1) * 128]
        return 0

    lax.fori_loop(0, 32, merge, 0, unroll=4)
    halves = []
    for n in range(2):
        r = u8[n, pl.ds(0, 256, stride=8), :]
        for t in range(1, 8):
            r = jnp.maximum(r, u8[n, pl.ds(t, 256, stride=8), :])
        halves.append(r.T)
    best = jnp.concatenate(halves, axis=0)
    prob = jnp.exp2(jnp.max(best.reshape(4, BLK, 256), axis=1))
    target = prob / jnp.sum(prob, axis=1, keepdims=True)
    me = z * YS + y
    tb[c, me, 0:4, :] = target[:, 0:128]
    tb[c, me, 4:8, :] = target[:, 128:256]
    mine = tb.at[c, me]
    for dz in (4, 3, 5, 2, 6, 1, 7, 0):
        for dy in (2, 1, 3, 0):
            if dz or dy:
                send(mine, mine, s_t, r_t.at[z], dev(zz(dz), yy(dy), c))

    o, kr = iota((112, 128), 0), iota((112, 128), 1)
    b = o % 4
    want_q = (b // 2) * 64 + (o % 16) // 4 * 16 + (o // 16) * 2 + b % 2
    want_i = (o % 16) // 4 * 16 + 10
    want_ii = (o % 8) // 2 * 16 + 10
    want = jnp.where(o < 80, want_q, jnp.where(o < 96, want_i, want_ii))
    pick = jnp.where(kr == want, 1.0, 0.0).astype(BF16)

    def unpack(i, _):
        cc, zi = i // ZS, lax.rem(i, ZS)
        rows = jnp.concatenate(
            [bufs[half][cc, zi, :, HALF:ROWS, :].reshape(64, HD) for half in range(2)], axis=0
        )
        got = mm(pick, rows)
        for g in range(GQ):
            pqb[g, i] = got[g * 16 : (g + 1) * 16].astype(BF16)
        posi[i] = got[80:96] + (iota((16, HD), 0) % 4).astype(F32)
        for half in range(2):
            at = 96 + half * 8
            posii[half, i] = got[at : at + 8] + (iota((8, HD), 0) % 2 + half * 2).astype(F32)
        return 0

    lax.fori_loop(0, 16, unpack, 0, unroll=4)
    pos_row = posi[...].reshape(256, HD)
    pos_col = posii[...].reshape(256, HD)
    pos_row = jnp.concatenate([pos_row, pos_row], axis=1)
    place = jnp.where(
        jnp.concatenate([pos_col, pos_col], axis=1) == iota((256, 256), 1).astype(F32), 1.0, 0.0
    ).astype(BF16)
    full = jnp.zeros((8, 256), F32)
    for term in split3(jnp.concatenate([target, target], axis=0)):
        full = full + mm(term, place)
    for n in range(4):
        map_ref[n] = full[n : n + 1]
    stores = [
        pltpu.make_async_copy(src, dst, s_out.at[n])
        for n, (src, dst) in enumerate(((map_ref, map_hbm), (gq_ref, gq_hbm), (gk_ref, gk_hbm)))
    ]
    stores[0].start()
    loads[4].wait()
    loads[5].wait()
    feats = kfb[...].reshape(256, 3 * HD).astype(BF16)
    gate_q = jnp.zeros((256, HD), F32)
    for g in range(GQ):
        gate_q = gate_q + mm(pqb[g].reshape(256, HD), wq_ref[0, g * HD : (g + 1) * HD, :])
    gate_q = gate_q.astype(BF16)
    gate_k = mm(feats, wk_ref[0]).astype(BF16)
    allowed = jnp.broadcast_to(pos_col.T[0:1, :], (256, 256)) <= pos_row
    logits = jnp.where(allowed, nt(gate_q, gate_k) * SCALE, NEG)
    shifted = logits - jnp.max(logits, axis=1, keepdims=True)
    log_prob = shifted - jnp.log(jnp.sum(jnp.exp(shifted), axis=1, keepdims=True))
    gqv[...] = gate_q
    gp[...] = jnp.exp(log_prob)
    lp[...] = jnp.where(allowed, log_prob, 0.0)

    def rows_of(cc):
        at = pl.ds(pl.multiple_of(cc * 128, 128), 128)
        tiles = tb[cc].reshape(16, 2, 8, 128)
        even, odd = tiles[:, 0], tiles[:, 1]
        low = iota((16, 8, 128), 1) < 4
        left = jnp.where(low, even, pltpu.roll(odd, 4, 1))
        right = jnp.where(low, pltpu.roll(even, 4, 1), odd)
        return at, jnp.concatenate([left.reshape(128, 128), right.reshape(128, 128)], axis=1)

    def terms(cc, at, targets):
        delta = (gp[at, :] - targets) * SCALE
        d_hi, d_lo = split2(delta)
        q_delta = jnp.concatenate(split2(mm(d_hi, gate_k) + mm(d_lo, gate_k)), axis=1)
        grads = []
        for g in range(GQ):
            pooled = pqb[g, pl.ds(pl.multiple_of(cc * ZS, ZS), ZS)].reshape(128, HD)
            both = tn(pooled, q_delta)
            grads.append(both[:, 0:HD] + both[:, HD:])
        return grads, tn(d_hi, gqv[at, :]) + tn(d_lo, gqv[at, :])

    for d in (0, 1, -1, 2, -2, 3, -3, 4):
        part = tb.at[c, pl.ds(zz(d) * YS, YS)]
        wait(tb.at[c, pl.ds(zz(d) * YS, YS if d else YS - 1)], r_t.at[zz(d)])
        send(part, part, s_ts, r_ts, sib)
    at, targets = rows_of(c)
    loss = -jnp.sum(targets * lp[at, :], axis=0, keepdims=True)
    loss = jnp.sum(loss, axis=1, keepdims=True)
    slot = c * XS + x
    lx[slot] = jnp.broadcast_to(loss, (8, 128))
    for peer in x_peers + [sib]:
        send(lx.at[slot], lx.at[slot], s_x, r_x, peer)
    near, k_near = terms(c, at, targets)
    for g in range(GQ):
        gq_ref[0, g * HD : (g + 1) * HD, :] = near[g]
    wait(tb.at[1 - c], r_ts)
    at, targets = rows_of(1 - c)
    far, k_far = terms(1 - c, at, targets)
    for g in range(GQ):
        gq_ref[0, g * HD : (g + 1) * HD, :] += far[g]
    stores[1].start()
    both = tn(feats, jnp.concatenate(split2(k_near + k_far), axis=1))
    gk_ref[0] = both[:, 0:HD] + both[:, HD:]
    stores[2].start()
    wait(lx.at[0:7], r_x)
    total = lx[0]
    for n in range(1, 2 * XS):
        total = total + lx[n]
    loss_ref[...] = total[0:1, 0:1] * (1.0 / (256 * XS))

    for store in stores:
        store.wait()
    wait(k0.at[c, 0, 0:3], s_y0)
    wait(k0.at[c, 0:7], s_z0)
    wait(k0.at[c], s_s0)
    wait(k1.at[c, 0:7, 0], s_z1)
    wait(k1.at[c, 0:6], s_y1)
    wait(k1.at[c], s_s1)
    wait(tb.at[c, 0:31], s_t)
    wait(tb.at[c], s_ts)
    wait(lx.at[0:7], s_x)


def place_results(
    map_in, gq_in, gk_in, loss_in, map_out, gq_out, gk_out, loss_out, map_v, gq_v, gk_v, sems
):
    through = ((gq_in, gq_v, gq_out), (gk_in, gk_v, gk_out), (map_in, map_v, map_out))
    into = [pltpu.make_async_copy(src, mid, sems.at[0, n]) for n, (src, mid, _) in enumerate(through)]
    out = [pltpu.make_async_copy(mid, dst, sems.at[1, n]) for n, (_, mid, dst) in enumerate(through)]
    for copy in into:
        copy.start()
    loss_out[...] = loss_in[...]
    for first, second in zip(into, out):
        first.wait()
        second.start()
    for copy in out:
        copy.wait()


def per_device(queries, keys, block_position, w_gate_q, w_gate_k):
    vmem = pl.BlockSpec(memory_space=pltpu.VMEM)
    smem = pl.BlockSpec(memory_space=pltpu.SMEM)
    hbm = pl.BlockSpec(memory_space=pltpu.HBM)
    dma = pltpu.SemaphoreType.DMA
    target_map, grad_q, grad_k, loss = pl.pallas_call(
        kernel,
        out_shape=(
            jax.ShapeDtypeStruct((4, 1, 256), F32),
            jax.ShapeDtypeStruct((1, GQ * HD, HD), F32),
            jax.ShapeDtypeStruct((1, 3 * HD, HD), F32),
            jax.ShapeDtypeStruct((1, 1), F32),
        ),
        in_specs=[hbm, hbm, smem, hbm, hbm],
        out_specs=(hbm, hbm, hbm, vmem),
        scratch_shapes=[
            pltpu.VMEM((4, 1, 256), F32),
            pltpu.VMEM((1, GQ * HD, HD), F32),
            pltpu.VMEM((1, 3 * HD, HD), F32),
            dma((3,)),
            pltpu.VMEM((TOK, GQ * HD), BF16),
            pltpu.VMEM((TOK, HD), BF16),
            pltpu.VMEM((1, GQ * HD, HD), BF16),
            pltpu.VMEM((1, 3 * HD, HD), BF16),
            pltpu.VMEM((2, ZS, YS, ROWS, HD), BF16),
            pltpu.VMEM((2, ZS, YS, ROWS, HD), BF16),
            pltpu.VMEM((GQ, 2 * HD, TOK), BF16),
            pltpu.VMEM((GQ, 2048, TOK), F32),
            pltpu.VMEM((GQ, 32, TOK), F32),
            pltpu.VMEM((GQ, 8, TOK), F32),
            pltpu.VMEM((GQ, 8, TOK), F32),
            pltpu.VMEM((8, 8, HD), F32),
            pltpu.VMEM((2, 2, ZS, 8, 3 * HD), F32),
            pltpu.VMEM((GQ, 16, 16, HD), BF16),
            pltpu.VMEM((16, 16, HD), F32),
            pltpu.VMEM((2, 16, 8, HD), F32),
            pltpu.VMEM((2, 2048, 128), F32),
            pltpu.VMEM((2, 32, 8, 128), F32),
            pltpu.VMEM((2 * XS, 8, 128), F32),
            pltpu.VMEM((256, 256), F32),
            pltpu.VMEM((256, 256), F32),
            pltpu.VMEM((256, HD), BF16),
            dma((6,)),
            dma, dma, dma, dma, dma, dma, dma, dma, dma,
            dma((3,)), dma((5, 2, 2)), dma((ZS,)), dma((5, 2)), dma((ZS,)), dma((ZS,)),
            dma((ZS,)), dma, dma,
        ],
        compiler_params=pltpu.CompilerParams(
            collective_id=0, has_side_effects=True, vmem_limit_bytes=63 << 20
        ),
        name="gate",
    )(queries, keys, block_position, w_gate_q, w_gate_k)
    hbm_out = (
        jax.ShapeDtypeStruct((4, 1, 256), F32),
        jax.ShapeDtypeStruct((1, GQ * HD, HD), F32),
        jax.ShapeDtypeStruct((1, 3 * HD, HD), F32),
        jax.ShapeDtypeStruct((1, 1), F32),
    )
    target_map, grad_q, grad_k, loss = pl.pallas_call(
        place_results,
        out_shape=hbm_out,
        in_specs=[hbm, hbm, hbm, vmem],
        out_specs=(hbm, hbm, hbm, vmem),
        scratch_shapes=[
            pltpu.VMEM((4, 1, 256), F32),
            pltpu.VMEM((1, GQ * HD, HD), F32),
            pltpu.VMEM((1, 3 * HD, HD), F32),
            dma((2, 3)),
        ],
        compiler_params=pltpu.CompilerParams(vmem_limit_bytes=63 << 20),
        name="place",
    )(target_map, grad_q, grad_k, loss)
    return target_map, grad_q, grad_k, loss.reshape(())


def solution(mesh):
    return jax.shard_map(
        per_device,
        mesh=mesh,
        in_specs=(
            P("ctx", "head"),
            P("ctx", "head"),
            P("ctx"),
            P("head", None, None),
            P("head", None, None),
        ),
        out_specs=(P("ctx", "head", None), P("head", None, None), P("head", None, None), P()),
        check_vma=False,
    )
```

```python
import functools
import math

import jax
import jax.numpy as jnp
from jax import lax
from jax.experimental import pallas as pl
from jax.experimental.pallas import tpu as pltpu
from jax.sharding import PartitionSpec as P

ZS, YS, XS = 8, 4, 4
BLK, HD, GQ = 64, 128, 5
TOK = 256
HALF = 128
ROWS = HALF + 16
NEG = -1e30
LOG2E = 1.4426950408889634
SCALE = 1.0 / math.sqrt(HD)
F32, BF16 = jnp.float32, jnp.bfloat16
MESH = pl.DeviceIdType.MESH


def nt(a, b):
    return lax.dot_general(a, b, (((1,), (1,)), ((), ())), preferred_element_type=F32)


def tn(a, b):
    return lax.dot_general(a, b, (((0,), (0,)), ((), ())), preferred_element_type=F32)


def mm(a, b):
    return jnp.dot(a, b, preferred_element_type=F32)


def split2(a):
    hi = a.astype(BF16)
    return hi, (a - hi.astype(F32)).astype(BF16)


def split3(a):
    hi, mid = split2(a)
    return hi, mid, (a - hi.astype(F32) - mid.astype(F32)).astype(BF16)


def iota(shape, dim):
    return lax.broadcasted_iota(jnp.int32, shape, dim)


def kernel(
    q_hbm, k_hbm, pos_hbm, wq_hbm, wk_hbm,
    map_hbm, gq_hbm, gk_hbm, loss_hbm,
    map_ref, gq_ref, gk_ref, loss_ref, pos_ref, s_out,
    q_ref, k_ref, wq_ref, wk_ref,
    k0, k1, qt, bm8, bmd, m8, l8, posv, kfb, pqb, posi, posii, u8, tb, lx, lp, gp, gqv, s_in,
    s_y0, s_z0, s_s0, s_z1, s_y1, s_s1, s_t, s_ts, s_x,
    r_y0, r_z0, r_s0, r_z1, r_y1, r_s1, r_t, r_ts, r_x,
):
    ctx, x = lax.axis_index("ctx"), lax.axis_index("head")
    c = lax.rem(ctx, 2)
    y = lax.rem(ctx // 2, YS)
    z = ctx // (2 * YS)

    def zz(d):
        return lax.rem(z + (d + ZS), ZS)

    def yy(d):
        return lax.rem(y + d, YS)

    def dev(z_at, y_at, c_at):
        return ((z_at * YS + y_at) * 2 + c_at, x)

    up, down, sib = dev(zz(1), y, c), dev(zz(-1), y, c), dev(z, y, 1 - c)
    y_peers = [dev(z, yy(d), c) for d in (1, 2, 3)]
    other = ctx + 1 - 2 * c
    x_peers = [(at, lax.rem(x + d, XS)) for d in (1, 2, 3) for at in (ctx, other)]

    barrier = pltpu.get_barrier_semaphore()
    peers = [up, down, sib] + y_peers + x_peers
    for peer in peers:
        pl.semaphore_signal(barrier, inc=1, device_id=peer, device_id_type=MESH)

    mine0, mine1 = k0.at[c, z, y], k1.at[c, z, y]
    own0, own1 = mine0.at[0:HALF], mine1.at[0:HALF]
    tile0, tile1 = mine0.at[HALF:ROWS], mine1.at[HALF:ROWS]
    keys0, keys1 = k_hbm.at[0:HALF], k_hbm.at[HALF:TOK]
    loads = [
        pltpu.make_async_copy(src, dst, s_in.at[n])
        for n, (src, dst) in enumerate(
            (
                (q_hbm, q_ref), (k_hbm, k_ref), (keys0, own0), (keys1, own1),
                (wq_hbm, wq_ref), (wk_hbm, wk_ref), (pos_hbm, pos_ref),
            )
        )
    ]
    for load in loads:
        load.start()
    def send(src, dst, s_sem, r_sem, to):
        pltpu.make_async_remote_copy(
            src_ref=src, dst_ref=dst, send_sem=s_sem, recv_sem=r_sem,
            device_id=to, device_id_type=MESH,
        ).start()

    def wait(like, sem):
        pltpu.make_async_copy(like, like, sem).wait()

    def send_own(src0, dst0, src1, dst1):
        for n, peer in enumerate(y_peers):
            send(src0, dst0, s_y0, r_y0.at[n], peer)
        for n, peer in ((0, up), (1, down)):
            send(src1, dst1, s_z1, r_z1.at[1, n], peer)
        for n, peer in ((0, up), (1, down)):
            send(src0, dst0, s_z0, r_z0.at[1, n, y // 2], peer)
        for peer in y_peers:
            send(src1, dst1, s_y1, r_y1.at[z], peer)

    pl.semaphore_wait(barrier, len(peers))
    send_own(keys0, own0, keys1, own1)

    loads[6].wait()
    first = pos_ref[0].astype(F32)
    loads[0].wait()
    row16 = iota((16, TOK), 0)
    tok16 = iota((16, TOK), 1)
    for half, tile in ((0, tile0), (1, tile1)):
        pooled = jnp.zeros((16, HD), F32)
        for g in range(GQ):
            pick = (row16 // 2 == g) & (tok16 // BLK == half * 2 + row16 % 2)
            weight = jnp.where(pick, 1.0 / BLK, 0.0).astype(BF16)
            pooled = pooled + mm(weight, q_ref[:, g * HD : (g + 1) * HD])
        pooled = jnp.where(iota((16, HD), 0) >= 10, first, pooled)
        tile[...] = pooled.astype(BF16)
    send_own(tile0, tile0, tile1, tile1)

    for g in range(GQ):
        scaled = (q_ref[:, g * HD : (g + 1) * HD].astype(F32) * (SCALE * LOG2E)).T
        hi, lo = split2(scaled)
        qt[g, 0:HD, :] = hi
        qt[g, HD : 2 * HD, :] = lo

    for n in (1, 2, 3):
        loads[n].wait()
    own_kk = jnp.concatenate([k_ref[...], k_ref[...]], axis=1)
    causal = iota((TOK, TOK), 0) <= iota((TOK, TOK), 1)
    for g in range(GQ):
        s = jnp.where(causal, mm(own_kk, qt[g]), NEG)
        m = jnp.max(s.reshape(4, 8, 8, TOK), axis=1)
        bmd[g] = m.reshape(32, TOK)
        top = jnp.max(m, axis=0)
        m8[g] = top
        l8[g] = jnp.sum(jnp.exp2(s.reshape(32, 8, TOK) - top[None]), axis=0)

    def z_pass(k):
        for n, src_z in ((0, zz(-k)), (1, zz(k))):
            part = k1.at[c, src_z, y]
            wait(part, r_z1.at[k, n])
            if k < 3:
                send(part, part, s_z1, r_z1.at[k + 1, n], up if n == 0 else down)
            else:
                @pl.when(c == n)
                def _(part=part, n=n):
                    send(part, part, s_z1, r_z1.at[4, 0], up if n == 0 else down)
            for peer in y_peers:
                send(part, part, s_y1, r_y1.at[src_z], peer)

    def y_done(d):
        at = zz(d)
        wait(k1.at[c, at, 0:3], r_y1.at[at])
        send(k1.at[c, at], k1.at[c, at], s_s1, r_s1.at[at], sib)

    def bundle_pass(k, p):
        pair = lax.rem(y // 2 + p, 2)
        for n, src_z in ((0, zz(-k)), (1, zz(k))):
            part = k0.at[c, src_z, pl.ds(2 * pair, 2)]
            wait(part, r_z0.at[k, n, pair])
            if k < 3:
                send(part, part, s_z0, r_z0.at[k + 1, n, pair], up if n == 0 else down)
            else:
                @pl.when(c == n)
                def _(part=part, n=n):
                    send(part, part, s_z0, r_z0.at[4, 0, pair], up if n == 0 else down)
        if p == 1:
            for src_z in (zz(-k), zz(k)):
                send(k0.at[c, src_z], k0.at[c, src_z], s_s0, r_s0.at[src_z], sib)

    def bundle_last():
        for pair in range(2):
            wait(k0.at[c, zz(4), 2 * pair : 2 * pair + 2], r_z0.at[4, 0, pair])
        whole = k0.at[c, zz(4)]
        send(whole, whole, s_s0, r_s0.at[zz(4)], sib)

    def z_last():
        part = k1.at[c, zz(4), y]
        wait(part, r_z1.at[4, 0])
        for peer in y_peers:
            send(part, part, s_y1, r_y1.at[zz(4)], peer)

    def y_pass(d):
        part = k0.at[c, z, yy(d)]
        wait(part, r_y0.at[3 - d])
        for n, peer in ((0, up), (1, down)):
            send(part, part, s_z0, r_z0.at[1, n, yy(d) // 2], peer)

    y_pass(3)
    y_pass(1)
    z_pass(1)
    y_pass(2)
    send(k0.at[c, z], k0.at[c, z], s_s0, r_s0.at[z], sib)
    y_done(0)

    bufs = (k0, k1)

    def attend(cc, zs):
        pieces = []
        for half in range(2):
            for zi in zs:
                piece = bufs[half][cc, zi, :, 0:HALF, :].reshape(YS * HALF, HD)
                wide = piece.astype(F32).reshape(8, BLK, HD)
                kfb[half, cc, zi, :, 0:HD] = jnp.max(wide, axis=1)
                kfb[half, cc, zi, :, HD : 2 * HD] = jnp.min(wide, axis=1)
                kfb[half, cc, zi, :, 2 * HD : 3 * HD] = jnp.sum(wide, axis=1) * (1.0 / BLK)
                pieces.append(piece)
        for n, zi in enumerate(zs):
            for yi in range(YS):
                mark = k0[cc, zi, yi, HALF:ROWS, :].astype(F32)[10:11, :]
                posv[n * YS + yi] = jnp.broadcast_to(mark, (8, HD))
        keys = jnp.concatenate(pieces, axis=0)
        kk = jnp.concatenate([keys, keys], axis=1)
        for g in range(GQ):
            s = mm(kk, qt[g])
            for side in range(2):
                cols = slice(side * 128, side * 128 + 128)
                top, total = m8[g, :, cols], l8[g, :, cols]
                for half in range(2):
                    for n, zi in enumerate(zs):
                        base = pl.multiple_of((half * 128 + (cc * ZS + zi) * 8) * 8, 64)
                        for yi in range(YS):
                            r0 = ((half * len(zs) + n) * YS + yi) * HALF
                            sb = s[r0 : r0 + HALF, cols].reshape(16, 8, 128)
                            ok = posv[n * YS + yi] < first
                            new = top
                            for blk in range(2):
                                m = jnp.max(sb[blk * 8 : blk * 8 + 8], axis=0)
                                m = jnp.where(ok, m, NEG)
                                bm8[g, pl.ds(base + (yi * 2 + blk) * 8, 8), cols] = m
                                new = jnp.maximum(new, m)
                            part = jnp.sum(jnp.exp2(sb - new[None]), axis=0)
                            total = total * jnp.exp2(top - new) + jnp.where(ok, part, 0.0)
                            top = new
                m8[g, :, cols] = top
                l8[g, :, cols] = total

    def both_cores(d):
        def one(j, _):
            cc = lax.rem(c + j, 2)

            @pl.when(j == 1)
            def _():
                if d == 0:
                    bundle_pass(1, 0)
                    z_pass(2)
                wait(k0.at[1 - c, zz(d)], r_s0.at[zz(d)])
                wait(k1.at[1 - c, zz(d)], r_s1.at[zz(d)])

            attend(cc, [zz(d)])
            return 0

        lax.fori_loop(0, 2, one, 0)

    def at_step(i, events):
        for number, event in events.items():
            @pl.when(i == number)
            def _(event=event):
                event()

    def pair_step(i, _):
        k, j = i // 2 + 1, lax.rem(i, 2)
        cc = lax.rem(c + j, 2)
        zs = [lax.rem(z + ZS - k, ZS), lax.rem(z + k, ZS)]
        at_step(i, {
            0: lambda: [bundle_pass(1, 1)] + [y_done(d) for d in (-1, 1)],
            1: lambda: [bundle_pass(2, 0), z_pass(3)],
            2: lambda: [bundle_pass(2, 1)] + [y_done(d) for d in (-2, 2)],
            3: lambda: [bundle_pass(3, 0), z_last()],
            4: lambda: [y_done(d) for d in (-3, 3)] + [bundle_pass(3, 1)],
            5: lambda: y_done(4),
        })

        @pl.when(j == 1)
        def _():
            for zi in zs:
                wait(k0.at[1 - c, zi], r_s0.at[zi])
                wait(k1.at[1 - c, zi], r_s1.at[zi])

        attend(cc, zs)
        return 0

    both_cores(0)
    lax.fori_loop(0, 6, pair_step, 0)
    bundle_last()
    both_cores(4)

    own = ((c * ZS + z) * YS + y) * 2
    for half in range(2):
        at = pl.multiple_of((half * 128 + own) * 8, 16)
        for g in range(GQ):
            bm8[g, pl.ds(at, 16), :] = bmd[g, half * 16 : half * 16 + 16, :]

    offs = []
    for g in range(GQ):
        m = jnp.max(m8[g], axis=0, keepdims=True)
        total = jnp.sum(l8[g] * jnp.exp2(m8[g] - m), axis=0, keepdims=True)
        offs.append(jnp.broadcast_to(m + jnp.log(total) * LOG2E, (8, TOK)))

    def merge(i, _):
        at = pl.multiple_of(i * 64, 64)
        best = None
        for g in range(GQ):
            v = bm8[g, pl.ds(at, 64), :].reshape(8, 8, TOK) - offs[g][None]
            best = v if best is None else jnp.maximum(best, v)
        best = best.reshape(64, TOK)
        for n in range(2):
            u8[n, pl.ds(at, 64), :] = best[:, n * 128 : (n + 1) * 128]
        return 0

    lax.fori_loop(0, 32, merge, 0, unroll=4)
    halves = []
    for n in range(2):
        r = u8[n, pl.ds(0, 256, stride=8), :]
        for t in range(1, 8):
            r = jnp.maximum(r, u8[n, pl.ds(t, 256, stride=8), :])
        halves.append(r.T)
    best = jnp.concatenate(halves, axis=0)
    prob = jnp.exp2(jnp.max(best.reshape(4, BLK, 256), axis=1))
    target = prob / jnp.sum(prob, axis=1, keepdims=True)
    me = z * YS + y
    tb[c, me, 0:4, :] = target[:, 0:128]
    tb[c, me, 4:8, :] = target[:, 128:256]
    mine = tb.at[c, me]
    for dz in (4, 3, 5, 2, 6, 1, 7, 0):
        for dy in (2, 1, 3, 0):
            if dz or dy:
                send(mine, mine, s_t, r_t.at[z], dev(zz(dz), yy(dy), c))

    o, kr = iota((112, 128), 0), iota((112, 128), 1)
    b = o % 4
    want_q = (b // 2) * 64 + (o % 16) // 4 * 16 + (o // 16) * 2 + b % 2
    want_i = (o % 16) // 4 * 16 + 10
    want_ii = (o % 8) // 2 * 16 + 10
    want = jnp.where(o < 80, want_q, jnp.where(o < 96, want_i, want_ii))
    pick = jnp.where(kr == want, 1.0, 0.0).astype(BF16)

    def unpack(i, _):
        cc, zi = i // ZS, lax.rem(i, ZS)
        rows = jnp.concatenate(
            [bufs[half][cc, zi, :, HALF:ROWS, :].reshape(64, HD) for half in range(2)], axis=0
        )
        got = mm(pick, rows)
        for g in range(GQ):
            pqb[g, i] = got[g * 16 : (g + 1) * 16].astype(BF16)
        posi[i] = got[80:96] + (iota((16, HD), 0) % 4).astype(F32)
        for half in range(2):
            at = 96 + half * 8
            posii[half, i] = got[at : at + 8] + (iota((8, HD), 0) % 2 + half * 2).astype(F32)
        return 0

    lax.fori_loop(0, 16, unpack, 0, unroll=4)
    pos_row = posi[...].reshape(256, HD)
    pos_col = posii[...].reshape(256, HD)
    pos_row = jnp.concatenate([pos_row, pos_row], axis=1)
    place = jnp.where(
        jnp.concatenate([pos_col, pos_col], axis=1) == iota((256, 256), 1).astype(F32), 1.0, 0.0
    ).astype(BF16)
    full = jnp.zeros((8, 256), F32)
    for term in split3(jnp.concatenate([target, target], axis=0)):
        full = full + mm(term, place)
    for n in range(4):
        map_ref[n] = full[n : n + 1]
    stores = [
        pltpu.make_async_copy(src, dst, s_out.at[n])
        for n, (src, dst) in enumerate(
            ((map_ref, map_hbm), (gq_ref, gq_hbm), (gk_ref, gk_hbm), (loss_ref, loss_hbm))
        )
    ]
    stores[0].start()
    loads[4].wait()
    loads[5].wait()
    feats = kfb[...].reshape(256, 3 * HD).astype(BF16)
    gate_q = jnp.zeros((256, HD), F32)
    for g in range(GQ):
        gate_q = gate_q + mm(pqb[g].reshape(256, HD), wq_ref[0, g * HD : (g + 1) * HD, :])
    gate_q = gate_q.astype(BF16)
    gate_k = mm(feats, wk_ref[0]).astype(BF16)
    allowed = jnp.broadcast_to(pos_col.T[0:1, :], (256, 256)) <= pos_row
    logits = jnp.where(allowed, nt(gate_q, gate_k) * SCALE, NEG)
    shifted = logits - jnp.max(logits, axis=1, keepdims=True)
    log_prob = shifted - jnp.log(jnp.sum(jnp.exp(shifted), axis=1, keepdims=True))
    gqv[...] = gate_q
    gp[...] = jnp.exp(log_prob)
    lp[...] = jnp.where(allowed, log_prob, 0.0)

    def rows_of(cc):
        at = pl.ds(pl.multiple_of(cc * 128, 128), 128)
        tiles = tb[cc].reshape(16, 2, 8, 128)
        even, odd = tiles[:, 0], tiles[:, 1]
        low = iota((16, 8, 128), 1) < 4
        left = jnp.where(low, even, pltpu.roll(odd, 4, 1))
        right = jnp.where(low, pltpu.roll(even, 4, 1), odd)
        return at, jnp.concatenate([left.reshape(128, 128), right.reshape(128, 128)], axis=1)

    def terms(cc, at, targets):
        delta = (gp[at, :] - targets) * SCALE
        d_hi, d_lo = split2(delta)
        q_delta = jnp.concatenate(split2(mm(d_hi, gate_k) + mm(d_lo, gate_k)), axis=1)
        grads = []
        for g in range(GQ):
            pooled = pqb[g, pl.ds(pl.multiple_of(cc * ZS, ZS), ZS)].reshape(128, HD)
            both = tn(pooled, q_delta)
            grads.append(both[:, 0:HD] + both[:, HD:])
        return grads, tn(d_hi, gqv[at, :]) + tn(d_lo, gqv[at, :])

    for d in (0, 1, -1, 2, -2, 3, -3, 4):
        part = tb.at[c, pl.ds(zz(d) * YS, YS)]
        wait(tb.at[c, pl.ds(zz(d) * YS, YS if d else YS - 1)], r_t.at[zz(d)])
        send(part, part, s_ts, r_ts, sib)
    at, targets = rows_of(c)
    loss = -jnp.sum(targets * lp[at, :], axis=0, keepdims=True)
    loss = jnp.sum(loss, axis=1, keepdims=True)
    slot = c * XS + x
    lx[slot] = jnp.broadcast_to(loss, (8, 128))
    for peer in x_peers + [sib]:
        send(lx.at[slot], lx.at[slot], s_x, r_x, peer)
    near, k_near = terms(c, at, targets)
    for g in range(GQ):
        gq_ref[0, g * HD : (g + 1) * HD, :] = near[g]
    wait(tb.at[1 - c], r_ts)
    at, targets = rows_of(1 - c)
    far, k_far = terms(1 - c, at, targets)
    for g in range(GQ):
        gq_ref[0, g * HD : (g + 1) * HD, :] += far[g]
    stores[1].start()
    both = tn(feats, jnp.concatenate(split2(k_near + k_far), axis=1))
    gk_ref[0] = both[:, 0:HD] + both[:, HD:]
    stores[2].start()
    wait(lx.at[0:7], r_x)
    total = lx[0]
    for n in range(1, 2 * XS):
        total = total + lx[n]
    loss_ref[...] = total[0:1, 0:1] * (1.0 / (256 * XS))
    stores[3].start()

    wait(k0.at[c, 0, 0:3], s_y0)
    wait(k0.at[c, 0:7], s_z0)
    wait(k0.at[c], s_s0)
    wait(k1.at[c, 0:7, 0], s_z1)
    wait(k1.at[c, 0:6], s_y1)
    wait(k1.at[c], s_s1)
    wait(tb.at[c, 0:31], s_t)
    wait(tb.at[c], s_ts)
    wait(lx.at[0:7], s_x)
    for store in stores:
        store.wait()


def place_results(
    map_in, gq_in, gk_in, loss_in, map_out, gq_out, gk_out, loss_out,
    map_v, gq_v, gk_v, loss_v, sems,
):
    through = (
        (gq_in, gq_v, gq_out), (gk_in, gk_v, gk_out),
        (map_in, map_v, map_out), (loss_in, loss_v, loss_out),
    )
    into = [pltpu.make_async_copy(src, mid, sems.at[0, n]) for n, (src, mid, _) in enumerate(through)]
    out = [pltpu.make_async_copy(mid, dst, sems.at[1, n]) for n, (_, mid, dst) in enumerate(through)]
    for copy in into:
        copy.start()
    for first, second in zip(into, out):
        first.wait()
        second.start()
    for copy in out:
        copy.wait()


def per_device(queries, keys, block_position, w_gate_q, w_gate_k):
    hbm = pl.BlockSpec(memory_space=pltpu.HBM)
    dma = pltpu.SemaphoreType.DMA
    target_map, grad_q, grad_k, loss = pl.pallas_call(
        kernel,
        out_shape=(
            jax.ShapeDtypeStruct((4, 1, 256), F32),
            jax.ShapeDtypeStruct((1, GQ * HD, HD), F32),
            jax.ShapeDtypeStruct((1, 3 * HD, HD), F32),
            jax.ShapeDtypeStruct((1, 1), F32),
        ),
        in_specs=[hbm, hbm, hbm, hbm, hbm],
        out_specs=(hbm, hbm, hbm, hbm),
        scratch_shapes=[
            pltpu.VMEM((4, 1, 256), F32),
            pltpu.VMEM((1, GQ * HD, HD), F32),
            pltpu.VMEM((1, 3 * HD, HD), F32),
            pltpu.VMEM((1, 1), F32),
            pltpu.SMEM((4,), jnp.int32),
            dma((4,)),
            pltpu.VMEM((TOK, GQ * HD), BF16),
            pltpu.VMEM((TOK, HD), BF16),
            pltpu.VMEM((1, GQ * HD, HD), BF16),
            pltpu.VMEM((1, 3 * HD, HD), BF16),
            pltpu.VMEM((2, ZS, YS, ROWS, HD), BF16),
            pltpu.VMEM((2, ZS, YS, ROWS, HD), BF16),
            pltpu.VMEM((GQ, 2 * HD, TOK), BF16),
            pltpu.VMEM((GQ, 2048, TOK), F32),
            pltpu.VMEM((GQ, 32, TOK), F32),
            pltpu.VMEM((GQ, 8, TOK), F32),
            pltpu.VMEM((GQ, 8, TOK), F32),
            pltpu.VMEM((8, 8, HD), F32),
            pltpu.VMEM((2, 2, ZS, 8, 3 * HD), F32),
            pltpu.VMEM((GQ, 16, 16, HD), BF16),
            pltpu.VMEM((16, 16, HD), F32),
            pltpu.VMEM((2, 16, 8, HD), F32),
            pltpu.VMEM((2, 2048, 128), F32),
            pltpu.VMEM((2, 32, 8, 128), F32),
            pltpu.VMEM((2 * XS, 8, 128), F32),
            pltpu.VMEM((256, 256), F32),
            pltpu.VMEM((256, 256), F32),
            pltpu.VMEM((256, HD), BF16),
            dma((7,)),
            dma, dma, dma, dma, dma, dma, dma, dma, dma,
            dma((3,)), dma((5, 2, 2)), dma((ZS,)), dma((5, 2)), dma((ZS,)), dma((ZS,)),
            dma((ZS,)), dma, dma,
        ],
        compiler_params=pltpu.CompilerParams(
            collective_id=0, has_side_effects=True, vmem_limit_bytes=63 << 20
        ),
        name="gate",
    )(queries, keys, block_position, w_gate_q, w_gate_k)
    hbm_out = (
        jax.ShapeDtypeStruct((4, 1, 256), F32),
        jax.ShapeDtypeStruct((1, GQ * HD, HD), F32),
        jax.ShapeDtypeStruct((1, 3 * HD, HD), F32),
        jax.ShapeDtypeStruct((1, 1), F32),
    )
    target_map, grad_q, grad_k, loss = pl.pallas_call(
        place_results,
        out_shape=hbm_out,
        in_specs=[hbm, hbm, hbm, hbm],
        out_specs=(hbm, hbm, hbm, hbm),
        scratch_shapes=[
            pltpu.VMEM((4, 1, 256), F32),
            pltpu.VMEM((1, GQ * HD, HD), F32),
            pltpu.VMEM((1, 3 * HD, HD), F32),
            pltpu.VMEM((1, 1), F32),
            dma((2, 4)),
        ],
        compiler_params=pltpu.CompilerParams(vmem_limit_bytes=63 << 20),
        name="place",
    )(target_map, grad_q, grad_k, loss)
    return target_map, grad_q, grad_k, loss.reshape(())


def solution(mesh):
    return jax.shard_map(
        per_device,
        mesh=mesh,
        in_specs=(
            P("ctx", "head"),
            P("ctx", "head"),
            P("ctx"),
            P("head", None, None),
            P("head", None, None),
        ),
        out_specs=(P("ctx", "head", None), P("head", None, None), P("head", None, None), P()),
        check_vma=False,
    )
```

```python
import functools
import math

import jax
import jax.numpy as jnp
from jax import lax
from jax.experimental import pallas as pl
from jax.experimental.pallas import tpu as pltpu
from jax.sharding import PartitionSpec as P

ZS, YS, XS = 8, 4, 4
BLK, HD, GQ = 64, 128, 5
TOK = 256
HALF = 128
ROWS = HALF + 16
NEG = -1e30
LOG2E = 1.4426950408889634
SCALE = 1.0 / math.sqrt(HD)
F32, BF16 = jnp.float32, jnp.bfloat16
MESH = pl.DeviceIdType.MESH


def nt(a, b):
    return lax.dot_general(a, b, (((1,), (1,)), ((), ())), preferred_element_type=F32)


def tn(a, b):
    return lax.dot_general(a, b, (((0,), (0,)), ((), ())), preferred_element_type=F32)


def mm(a, b):
    return jnp.dot(a, b, preferred_element_type=F32)


def split2(a):
    hi = a.astype(BF16)
    return hi, (a - hi.astype(F32)).astype(BF16)


def split3(a):
    hi, mid = split2(a)
    return hi, mid, (a - hi.astype(F32) - mid.astype(F32)).astype(BF16)


def iota(shape, dim):
    return lax.broadcasted_iota(jnp.int32, shape, dim)


def kernel(
    q_hbm, k_hbm, pos_hbm, wq_hbm, wk_hbm,
    map_hbm, gq_hbm, gk_hbm, loss_hbm,
    map_ref, gq_ref, gk_ref, loss_ref, pos_ref, s_out,
    q_ref, k_ref, wq_ref, wk_ref,
    k0, k1, qt, bm8, bmd, m8, l8, posv, kfb, pqb, posi, posii, u8, tb, lx, lp, gp, gqv, s_in,
    s_y0, s_z0, s_s0, s_z1, s_y1, s_s1, s_t, s_ts, s_x,
    r_y0, r_z0, r_s0, r_z1, r_y1, r_s1, r_t, r_ts, r_x,
):
    ctx, x = lax.axis_index("ctx"), lax.axis_index("head")
    c = lax.rem(ctx, 2)
    y = lax.rem(ctx // 2, YS)
    z = ctx // (2 * YS)

    def zz(d):
        return lax.rem(z + (d + ZS), ZS)

    def yy(d):
        return lax.rem(y + d, YS)

    def dev(z_at, y_at, c_at):
        return ((z_at * YS + y_at) * 2 + c_at, x)

    up, down, sib = dev(zz(1), y, c), dev(zz(-1), y, c), dev(z, y, 1 - c)
    y_peers = [dev(z, yy(d), c) for d in (1, 2, 3)]
    other = ctx + 1 - 2 * c
    x_peers = [(at, lax.rem(x + d, XS)) for d in (1, 2, 3) for at in (ctx, other)]

    barrier = pltpu.get_barrier_semaphore()
    peers = [up, down, sib] + y_peers + x_peers
    for peer in peers:
        pl.semaphore_signal(barrier, inc=1, device_id=peer, device_id_type=MESH)

    mine0, mine1 = k0.at[c, z, y], k1.at[c, z, y]
    own0, own1 = mine0.at[0:HALF], mine1.at[0:HALF]
    tile0, tile1 = mine0.at[HALF:ROWS], mine1.at[HALF:ROWS]
    keys0, keys1 = k_hbm.at[0:HALF], k_hbm.at[HALF:TOK]
    loads = [
        pltpu.make_async_copy(src, dst, s_in.at[n])
        for n, (src, dst) in enumerate(
            (
                (q_hbm, q_ref), (k_hbm, k_ref), (keys0, own0), (keys1, own1),
                (wq_hbm, wq_ref), (wk_hbm, wk_ref), (pos_hbm, pos_ref),
            )
        )
    ]
    for load in loads:
        load.start()
    def send(src, dst, s_sem, r_sem, to):
        pltpu.make_async_remote_copy(
            src_ref=src, dst_ref=dst, send_sem=s_sem, recv_sem=r_sem,
            device_id=to, device_id_type=MESH,
        ).start()

    def wait(like, sem):
        pltpu.make_async_copy(like, like, sem).wait()

    def send_own(src0, dst0, src1, dst1):
        for n, peer in enumerate(y_peers):
            send(src0, dst0, s_y0, r_y0.at[n], peer)
        for n, peer in ((0, up), (1, down)):
            send(src1, dst1, s_z1, r_z1.at[1, n], peer)
        for n, peer in ((0, up), (1, down)):
            send(src0, dst0, s_z0, r_z0.at[1, n, y // 2], peer)
        for peer in y_peers:
            send(src1, dst1, s_y1, r_y1.at[z], peer)

    pl.semaphore_wait(barrier, len(peers))
    send_own(keys0, own0, keys1, own1)

    loads[6].wait()
    first = pos_ref[0].astype(F32)
    loads[0].wait()
    row16 = iota((16, TOK), 0)
    tok16 = iota((16, TOK), 1)
    for half, tile in ((0, tile0), (1, tile1)):
        pooled = jnp.zeros((16, HD), F32)
        for g in range(GQ):
            pick = (row16 // 2 == g) & (tok16 // BLK == half * 2 + row16 % 2)
            weight = jnp.where(pick, 1.0 / BLK, 0.0).astype(BF16)
            pooled = pooled + mm(weight, q_ref[:, g * HD : (g + 1) * HD])
        pooled = jnp.where(iota((16, HD), 0) >= 10, first, pooled)
        tile[...] = pooled.astype(BF16)
    send_own(tile0, tile0, tile1, tile1)

    for g in range(GQ):
        scaled = (q_ref[:, g * HD : (g + 1) * HD].astype(F32) * (SCALE * LOG2E)).T
        hi, lo = split2(scaled)
        qt[g, 0:HD, :] = hi
        qt[g, HD : 2 * HD, :] = lo

    for n in (1, 2, 3):
        loads[n].wait()
    own_kk = jnp.concatenate([k_ref[...], k_ref[...]], axis=1)
    causal = iota((TOK, TOK), 0) <= iota((TOK, TOK), 1)
    for g in range(GQ):
        s = jnp.where(causal, mm(own_kk, qt[g]), NEG)
        m = jnp.max(s.reshape(4, 8, 8, TOK), axis=1)
        bmd[g] = m.reshape(32, TOK)
        top = jnp.max(m, axis=0)
        m8[g] = top
        l8[g] = jnp.sum(jnp.exp2(s.reshape(32, 8, TOK) - top[None]), axis=0)

    def z_pass(k):
        for n, src_z in ((0, zz(-k)), (1, zz(k))):
            part = k1.at[c, src_z, y]
            wait(part, r_z1.at[k, n])
            if k < 3:
                send(part, part, s_z1, r_z1.at[k + 1, n], up if n == 0 else down)
            else:
                @pl.when(c == n)
                def _(part=part, n=n):
                    send(part, part, s_z1, r_z1.at[4, 0], up if n == 0 else down)
            for peer in y_peers:
                send(part, part, s_y1, r_y1.at[src_z], peer)

    def y_done(d):
        at = zz(d)
        wait(k1.at[c, at, 0:3], r_y1.at[at])
        send(k1.at[c, at], k1.at[c, at], s_s1, r_s1.at[at], sib)

    def bundle_pass(k, p):
        pair = lax.rem(y // 2 + p, 2)
        for n, src_z in ((0, zz(-k)), (1, zz(k))):
            part = k0.at[c, src_z, pl.ds(2 * pair, 2)]
            wait(part, r_z0.at[k, n, pair])
            if k < 3:
                send(part, part, s_z0, r_z0.at[k + 1, n, pair], up if n == 0 else down)
            else:
                @pl.when(c == n)
                def _(part=part, n=n):
                    send(part, part, s_z0, r_z0.at[4, 0, pair], up if n == 0 else down)
        if p == 1:
            for src_z in (zz(-k), zz(k)):
                send(k0.at[c, src_z], k0.at[c, src_z], s_s0, r_s0.at[src_z], sib)

    def bundle_last():
        for pair in range(2):
            wait(k0.at[c, zz(4), 2 * pair : 2 * pair + 2], r_z0.at[4, 0, pair])
        whole = k0.at[c, zz(4)]
        send(whole, whole, s_s0, r_s0.at[zz(4)], sib)

    def z_last():
        part = k1.at[c, zz(4), y]
        wait(part, r_z1.at[4, 0])
        for peer in y_peers:
            send(part, part, s_y1, r_y1.at[zz(4)], peer)

    def y_pass(d):
        part = k0.at[c, z, yy(d)]
        wait(part, r_y0.at[3 - d])
        for n, peer in ((0, up), (1, down)):
            send(part, part, s_z0, r_z0.at[1, n, yy(d) // 2], peer)

    y_pass(3)
    y_pass(1)
    z_pass(1)
    y_pass(2)
    send(k0.at[c, z], k0.at[c, z], s_s0, r_s0.at[z], sib)
    y_done(0)

    bufs = (k0, k1)

    def attend(cc, zs):
        pieces = []
        for half in range(2):
            for zi in zs:
                piece = bufs[half][cc, zi, :, 0:HALF, :].reshape(YS * HALF, HD)
                wide = piece.astype(F32).reshape(8, BLK, HD)
                kfb[half, cc, zi, :, 0:HD] = jnp.max(wide, axis=1)
                kfb[half, cc, zi, :, HD : 2 * HD] = jnp.min(wide, axis=1)
                kfb[half, cc, zi, :, 2 * HD : 3 * HD] = jnp.sum(wide, axis=1) * (1.0 / BLK)
                pieces.append(piece)
        for n, zi in enumerate(zs):
            for yi in range(YS):
                mark = k0[cc, zi, yi, HALF:ROWS, :].astype(F32)[10:11, :]
                posv[n * YS + yi] = jnp.broadcast_to(mark, (8, HD))
        keys = jnp.concatenate(pieces, axis=0)
        kk = jnp.concatenate([keys, keys], axis=1)
        for g in range(GQ):
            s = mm(kk, qt[g])
            for side in range(2):
                cols = slice(side * 128, side * 128 + 128)
                top, total = m8[g, :, cols], l8[g, :, cols]
                for half in range(2):
                    for n, zi in enumerate(zs):
                        base = pl.multiple_of((half * 128 + (cc * ZS + zi) * 8) * 8, 64)
                        for yi in range(YS):
                            r0 = ((half * len(zs) + n) * YS + yi) * HALF
                            sb = s[r0 : r0 + HALF, cols].reshape(16, 8, 128)
                            ok = posv[n * YS + yi] < first
                            new = top
                            for blk in range(2):
                                m = jnp.max(sb[blk * 8 : blk * 8 + 8], axis=0)
                                m = jnp.where(ok, m, NEG)
                                bm8[g, pl.ds(base + (yi * 2 + blk) * 8, 8), cols] = m
                                new = jnp.maximum(new, m)
                            part = jnp.sum(jnp.exp2(sb - new[None]), axis=0)
                            total = total * jnp.exp2(top - new) + jnp.where(ok, part, 0.0)
                            top = new
                m8[g, :, cols] = top
                l8[g, :, cols] = total

    def both_cores(d):
        def one(j, _):
            cc = lax.rem(c + j, 2)

            @pl.when(j == 1)
            def _():
                if d == 0:
                    bundle_pass(1, 0)
                    z_pass(2)
                wait(k0.at[1 - c, zz(d)], r_s0.at[zz(d)])
                wait(k1.at[1 - c, zz(d)], r_s1.at[zz(d)])

            attend(cc, [zz(d)])
            return 0

        lax.fori_loop(0, 2, one, 0)

    def at_step(i, events):
        for number, event in events.items():
            @pl.when(i == number)
            def _(event=event):
                event()

    def pair_step(i, _):
        k, j = i // 2 + 1, lax.rem(i, 2)
        cc = lax.rem(c + j, 2)
        zs = [lax.rem(z + ZS - k, ZS), lax.rem(z + k, ZS)]
        at_step(i, {
            0: lambda: [bundle_pass(1, 1)] + [y_done(d) for d in (-1, 1)],
            1: lambda: [bundle_pass(2, 0), z_pass(3)],
            2: lambda: [bundle_pass(2, 1)] + [y_done(d) for d in (-2, 2)],
            3: lambda: [bundle_pass(3, 0), z_last()],
            4: lambda: [y_done(d) for d in (-3, 3)] + [bundle_pass(3, 1)],
            5: lambda: y_done(4),
        })

        @pl.when(j == 1)
        def _():
            for zi in zs:
                wait(k0.at[1 - c, zi], r_s0.at[zi])
                wait(k1.at[1 - c, zi], r_s1.at[zi])

        attend(cc, zs)
        return 0

    both_cores(0)
    lax.fori_loop(0, 6, pair_step, 0)
    bundle_last()
    both_cores(4)

    own = ((c * ZS + z) * YS + y) * 2
    for half in range(2):
        at = pl.multiple_of((half * 128 + own) * 8, 16)
        for g in range(GQ):
            bm8[g, pl.ds(at, 16), :] = bmd[g, half * 16 : half * 16 + 16, :]

    offs = []
    for g in range(GQ):
        m = jnp.max(m8[g], axis=0, keepdims=True)
        total = jnp.sum(l8[g] * jnp.exp2(m8[g] - m), axis=0, keepdims=True)
        offs.append(jnp.broadcast_to(m + jnp.log(total) * LOG2E, (8, TOK)))

    def merge(i, _):
        at = pl.multiple_of(i * 64, 64)
        best = None
        for g in range(GQ):
            v = bm8[g, pl.ds(at, 64), :].reshape(8, 8, TOK) - offs[g][None]
            best = v if best is None else jnp.maximum(best, v)
        best = best.reshape(64, TOK)
        for n in range(2):
            u8[n, pl.ds(at, 64), :] = best[:, n * 128 : (n + 1) * 128]
        return 0

    lax.fori_loop(0, 32, merge, 0, unroll=8)
    halves = []
    for n in range(2):
        r = u8[n, pl.ds(0, 256, stride=8), :]
        for t in range(1, 8):
            r = jnp.maximum(r, u8[n, pl.ds(t, 256, stride=8), :])
        halves.append(r.T)
    best = jnp.concatenate(halves, axis=0)
    prob = jnp.exp2(jnp.max(best.reshape(4, BLK, 256), axis=1))
    target = prob / jnp.sum(prob, axis=1, keepdims=True)
    me = z * YS + y
    tb[c, me, 0:4, :] = target[:, 0:128]
    tb[c, me, 4:8, :] = target[:, 128:256]
    mine = tb.at[c, me]
    for dz in (4, 3, 5, 2, 6, 1, 7, 0):
        for dy in (2, 1, 3, 0):
            if dz or dy:
                send(mine, mine, s_t, r_t.at[z], dev(zz(dz), yy(dy), c))

    o, kr = iota((112, 128), 0), iota((112, 128), 1)
    b = o % 4
    want_q = (b // 2) * 64 + (o % 16) // 4 * 16 + (o // 16) * 2 + b % 2
    want_i = (o % 16) // 4 * 16 + 10
    want_ii = (o % 8) // 2 * 16 + 10
    want = jnp.where(o < 80, want_q, jnp.where(o < 96, want_i, want_ii))
    pick = jnp.where(kr == want, 1.0, 0.0).astype(BF16)

    def unpack(i, _):
        cc, zi = i // ZS, lax.rem(i, ZS)
        rows = jnp.concatenate(
            [bufs[half][cc, zi, :, HALF:ROWS, :].reshape(64, HD) for half in range(2)], axis=0
        )
        got = mm(pick, rows)
        for g in range(GQ):
            pqb[g, i] = got[g * 16 : (g + 1) * 16].astype(BF16)
        posi[i] = got[80:96] + (iota((16, HD), 0) % 4).astype(F32)
        for half in range(2):
            at = 96 + half * 8
            posii[half, i] = got[at : at + 8] + (iota((8, HD), 0) % 2 + half * 2).astype(F32)
        return 0

    lax.fori_loop(0, 16, unpack, 0, unroll=4)
    pos_row = posi[...].reshape(256, HD)
    pos_col = posii[...].reshape(256, HD)
    pos_row = jnp.concatenate([pos_row, pos_row], axis=1)
    place = jnp.where(
        jnp.concatenate([pos_col, pos_col], axis=1) == iota((256, 256), 1).astype(F32), 1.0, 0.0
    ).astype(BF16)
    full = jnp.zeros((8, 256), F32)
    for term in split3(jnp.concatenate([target, target], axis=0)):
        full = full + mm(term, place)
    for n in range(4):
        map_ref[n] = full[n : n + 1]
    stores = [
        pltpu.make_async_copy(src, dst, s_out.at[n])
        for n, (src, dst) in enumerate(
            ((map_ref, map_hbm), (gq_ref, gq_hbm), (gk_ref, gk_hbm), (loss_ref, loss_hbm))
        )
    ]
    stores[0].start()
    loads[4].wait()
    loads[5].wait()
    feats = kfb[...].reshape(256, 3 * HD).astype(BF16)
    gate_q = jnp.zeros((256, HD), F32)
    for g in range(GQ):
        gate_q = gate_q + mm(pqb[g].reshape(256, HD), wq_ref[0, g * HD : (g + 1) * HD, :])
    gate_q = gate_q.astype(BF16)
    gate_k = mm(feats, wk_ref[0]).astype(BF16)
    allowed = jnp.broadcast_to(pos_col.T[0:1, :], (256, 256)) <= pos_row
    logits = jnp.where(allowed, nt(gate_q, gate_k) * SCALE, NEG)
    shifted = logits - jnp.max(logits, axis=1, keepdims=True)
    log_prob = shifted - jnp.log(jnp.sum(jnp.exp(shifted), axis=1, keepdims=True))
    gqv[...] = gate_q
    gp[...] = jnp.exp(log_prob)
    lp[...] = jnp.where(allowed, log_prob, 0.0)

    def rows_of(cc):
        at = pl.ds(pl.multiple_of(cc * 128, 128), 128)
        tiles = tb[cc].reshape(16, 2, 8, 128)
        even, odd = tiles[:, 0], tiles[:, 1]
        low = iota((16, 8, 128), 1) < 4
        left = jnp.where(low, even, pltpu.roll(odd, 4, 1))
        right = jnp.where(low, pltpu.roll(even, 4, 1), odd)
        return at, jnp.concatenate([left.reshape(128, 128), right.reshape(128, 128)], axis=1)

    def terms(cc, at, targets):
        delta = (gp[at, :] - targets) * SCALE
        d_hi, d_lo = split2(delta)
        q_delta = jnp.concatenate(split2(mm(d_hi, gate_k) + mm(d_lo, gate_k)), axis=1)
        grads = []
        for g in range(GQ):
            pooled = pqb[g, pl.ds(pl.multiple_of(cc * ZS, ZS), ZS)].reshape(128, HD)
            both = tn(pooled, q_delta)
            grads.append(both[:, 0:HD] + both[:, HD:])
        return grads, tn(d_hi, gqv[at, :]) + tn(d_lo, gqv[at, :])

    for d in (0, 1, -1, 2, -2, 3, -3, 4):
        part = tb.at[c, pl.ds(zz(d) * YS, YS)]
        wait(tb.at[c, pl.ds(zz(d) * YS, YS if d else YS - 1)], r_t.at[zz(d)])
        send(part, part, s_ts, r_ts, sib)
    at, targets = rows_of(c)
    loss = -jnp.sum(targets * lp[at, :], axis=0, keepdims=True)
    loss = jnp.sum(loss, axis=1, keepdims=True)
    slot = c * XS + x
    lx[slot] = jnp.broadcast_to(loss, (8, 128))
    for peer in x_peers + [sib]:
        send(lx.at[slot], lx.at[slot], s_x, r_x, peer)
    near, k_near = terms(c, at, targets)
    for g in range(GQ):
        gq_ref[0, g * HD : (g + 1) * HD, :] = near[g]
    wait(tb.at[1 - c], r_ts)
    at, targets = rows_of(1 - c)
    far, k_far = terms(1 - c, at, targets)
    for g in range(GQ):
        gq_ref[0, g * HD : (g + 1) * HD, :] += far[g]
    stores[1].start()
    both = tn(feats, jnp.concatenate(split2(k_near + k_far), axis=1))
    gk_ref[0] = both[:, 0:HD] + both[:, HD:]
    stores[2].start()
    wait(lx.at[0:7], r_x)
    total = lx[0]
    for n in range(1, 2 * XS):
        total = total + lx[n]
    loss_ref[...] = total[0:1, 0:1] * (1.0 / (256 * XS))
    stores[3].start()

    wait(k0.at[c, 0, 0:3], s_y0)
    wait(k0.at[c, 0:7], s_z0)
    wait(k0.at[c], s_s0)
    wait(k1.at[c, 0:7, 0], s_z1)
    wait(k1.at[c, 0:6], s_y1)
    wait(k1.at[c], s_s1)
    wait(tb.at[c, 0:31], s_t)
    wait(tb.at[c], s_ts)
    wait(lx.at[0:7], s_x)
    for store in stores:
        store.wait()


def place_results(
    map_in, gq_in, gk_in, loss_in, map_out, gq_out, gk_out, loss_out,
    map_v, gq_v, gk_v, loss_v, sems,
):
    half = pl.ds(0, GQ * HD // 2), pl.ds(GQ * HD // 2, GQ * HD // 2)
    through = (
        (loss_in, loss_v, loss_out), (map_in, map_v, map_out), (gk_in, gk_v, gk_out),
        (gq_in.at[:, half[0]], gq_v.at[:, half[0]], gq_out.at[:, half[0]]),
        (gq_in.at[:, half[1]], gq_v.at[:, half[1]], gq_out.at[:, half[1]]),
    )
    into = [pltpu.make_async_copy(src, mid, sems.at[0, n]) for n, (src, mid, _) in enumerate(through)]
    out = [pltpu.make_async_copy(mid, dst, sems.at[1, n]) for n, (_, mid, dst) in enumerate(through)]
    for copy in into:
        copy.start()
    for first, second in zip(into, out):
        first.wait()
        second.start()
    for copy in out:
        copy.wait()


def per_device(queries, keys, block_position, w_gate_q, w_gate_k):
    hbm = pl.BlockSpec(memory_space=pltpu.HBM)
    dma = pltpu.SemaphoreType.DMA
    target_map, grad_q, grad_k, loss = pl.pallas_call(
        kernel,
        out_shape=(
            jax.ShapeDtypeStruct((4, 1, 256), F32),
            jax.ShapeDtypeStruct((1, GQ * HD, HD), F32),
            jax.ShapeDtypeStruct((1, 3 * HD, HD), F32),
            jax.ShapeDtypeStruct((1, 1), F32),
        ),
        in_specs=[hbm, hbm, hbm, hbm, hbm],
        out_specs=(hbm, hbm, hbm, hbm),
        scratch_shapes=[
            pltpu.VMEM((4, 1, 256), F32),
            pltpu.VMEM((1, GQ * HD, HD), F32),
            pltpu.VMEM((1, 3 * HD, HD), F32),
            pltpu.VMEM((1, 1), F32),
            pltpu.SMEM((4,), jnp.int32),
            dma((4,)),
            pltpu.VMEM((TOK, GQ * HD), BF16),
            pltpu.VMEM((TOK, HD), BF16),
            pltpu.VMEM((1, GQ * HD, HD), BF16),
            pltpu.VMEM((1, 3 * HD, HD), BF16),
            pltpu.VMEM((2, ZS, YS, ROWS, HD), BF16),
            pltpu.VMEM((2, ZS, YS, ROWS, HD), BF16),
            pltpu.VMEM((GQ, 2 * HD, TOK), BF16),
            pltpu.VMEM((GQ, 2048, TOK), F32),
            pltpu.VMEM((GQ, 32, TOK), F32),
            pltpu.VMEM((GQ, 8, TOK), F32),
            pltpu.VMEM((GQ, 8, TOK), F32),
            pltpu.VMEM((8, 8, HD), F32),
            pltpu.VMEM((2, 2, ZS, 8, 3 * HD), F32),
            pltpu.VMEM((GQ, 16, 16, HD), BF16),
            pltpu.VMEM((16, 16, HD), F32),
            pltpu.VMEM((2, 16, 8, HD), F32),
            pltpu.VMEM((2, 2048, 128), F32),
            pltpu.VMEM((2, 32, 8, 128), F32),
            pltpu.VMEM((2 * XS, 8, 128), F32),
            pltpu.VMEM((256, 256), F32),
            pltpu.VMEM((256, 256), F32),
            pltpu.VMEM((256, HD), BF16),
            dma((7,)),
            dma, dma, dma, dma, dma, dma, dma, dma, dma,
            dma((3,)), dma((5, 2, 2)), dma((ZS,)), dma((5, 2)), dma((ZS,)), dma((ZS,)),
            dma((ZS,)), dma, dma,
        ],
        compiler_params=pltpu.CompilerParams(
            collective_id=0, has_side_effects=True, vmem_limit_bytes=63 << 20
        ),
        name="gate",
    )(queries, keys, block_position, w_gate_q, w_gate_k)
    hbm_out = (
        jax.ShapeDtypeStruct((4, 1, 256), F32),
        jax.ShapeDtypeStruct((1, GQ * HD, HD), F32),
        jax.ShapeDtypeStruct((1, 3 * HD, HD), F32),
        jax.ShapeDtypeStruct((1, 1), F32),
    )
    target_map, grad_q, grad_k, loss = pl.pallas_call(
        place_results,
        out_shape=hbm_out,
        in_specs=[hbm, hbm, hbm, hbm],
        out_specs=(hbm, hbm, hbm, hbm),
        scratch_shapes=[
            pltpu.VMEM((4, 1, 256), F32),
            pltpu.VMEM((1, GQ * HD, HD), F32),
            pltpu.VMEM((1, 3 * HD, HD), F32),
            pltpu.VMEM((1, 1), F32),
            dma((2, 5)),
        ],
        compiler_params=pltpu.CompilerParams(vmem_limit_bytes=63 << 20),
        name="place",
    )(target_map, grad_q, grad_k, loss)
    return target_map, grad_q, grad_k, loss.reshape(())


def solution(mesh):
    return jax.shard_map(
        per_device,
        mesh=mesh,
        in_specs=(
            P("ctx", "head"),
            P("ctx", "head"),
            P("ctx"),
            P("head", None, None),
            P("head", None, None),
        ),
        out_specs=(P("ctx", "head", None), P("head", None, None), P("head", None, None), P()),
        check_vma=False,
    )
```
